32 devices in a mesh: aux: 8 (over z, y), pair: 4 (over x, core).
Axes of the slice: x: 2, y: 2, z: 4, core: 2. Of those that a mesh axis runs over, the one named last changes fastest.
Arguments:
- half_ints: bfloat16 [24, 1408, 4096], P('pair', None, 'aux'), may hold values from -0.75 to 0.75
- vir_coeffs: bfloat16 [1408, 1280], P(None, 'aux'), may hold values from -0.15625 to 0.15625
- occ_energy: float32 [24], replicated, may hold values from -2 to -0.3
- vir_energy: float32 [1280], replicated, may hold values from 0.3 to 4
- roster: int32 [8, 2], replicated, may hold values from 0 to 3
Outputs:
- density: bfloat16 [1280, 24, 4096], P('pair', 'aux')
The draws below stay inside these ranges and needn't reach their ends.
All inputs are finite; a program needn't handle non-finite values.
Results may differ from the reference program's by a relative error of at most 0.0058.
Values may be sent and summed in bfloat16 or wider, within the bound.
No kernel may reach another device: no remote copies, remote signals or barrier semaphores. Data moves between devices by JAX's collectives and lax.ppermute only.
A program may use at most 128 MiB of HBM per device.

```python
import jax
import jax.numpy as jnp
from jax import lax

N = 1408
V = 1280
P_SIZE = 4096
OCC_BLK = 3
STEPS = 2
OCC = 24
VBLOCKS = 4
N_AUX = 8
N_PAIR = 4


def place_ends(array, rng, low, largest):
    place = [jax.random.randint(jax.random.fold_in(rng, axis), (), 0, length) for axis, length in enumerate(array.shape)]
    widest = array.shape.index(max(array.shape))
    next_to = place[:widest] + [(place[widest] + 1) % array.shape[widest]] + place[widest + 1:]
    return array.at[tuple(place)].set(low).at[tuple(next_to)].set(largest)


def level_of(rng, dims, cuts, low, top_value):
    factor_of = 1.0
    for dim, parts in cuts:
        steps = jax.random.uniform(jax.random.fold_in(jax.random.fold_in(rng, 6), dim), (parts,), jnp.float32, low / len(cuts), top_value / len(cuts))
        factor_of = factor_of * jnp.repeat(jnp.exp(steps), dims[dim] // parts).reshape((-1,) + (1,) * (len(dims) - 1 - dim))
    return factor_of


def normal_values(stream_key, shape, scale, reach, cuts=(), kind=jnp.bfloat16):
    factor_of = level_of(stream_key, shape, cuts, -0.22, 0.18) if cuts else 1.0
    values = jax.random.normal(stream_key, shape, jnp.float32) * scale * factor_of
    return jnp.minimum(jnp.maximum(values, -reach), reach).astype(kind)


def setup_inputs(seed: int = 0) -> dict:
    splits = jax.random.split(jax.random.key(seed), 6)
    half_ints = normal_values(splits[0], (OCC, N, P_SIZE), 0.125, 0.75, ((0, 4), (2, 8)))
    vir_coeffs = normal_values(splits[1], (N, V), N ** -0.5, 0.15625, ((1, 8),))
    occ_energy = jnp.clip(jax.random.uniform(splits[2], (OCC,), jnp.float32, -2.0, -0.3), -2.0, -0.3)
    vir_energy = jnp.clip(jax.random.uniform(splits[3], (V,), jnp.float32, 0.3, 4.0), 0.3, 4.0)
    roster = place_ends(jax.random.randint(splits[4], (OCC // OCC_BLK, STEPS), 0, VBLOCKS), jax.random.fold_in(splits[4], 1), 0, VBLOCKS - 1).astype(jnp.int32)
    return dict(half_ints=half_ints, vir_coeffs=vir_coeffs, occ_energy=occ_energy, vir_energy=vir_energy, roster=roster)


spin_scale = 1.3


def reference(half_ints, vir_coeffs, occ_energy, vir_energy, roster):
    vir_width = V // N_PAIR
    coeff_rows = jnp.transpose(vir_coeffs)

    def one_block(block_index):
        row_start = (block_index * OCC_BLK).astype(jnp.int32)
        half_block = lax.dynamic_slice_in_dim(half_ints, row_start, OCC_BLK, 0)
        half_flat = jnp.transpose(half_block, (1, 0, 2)).reshape(N, OCC_BLK * P_SIZE)
        vir_ints = jnp.dot(coeff_rows, half_flat, preferred_element_type=jnp.float32).astype(jnp.bfloat16).reshape(V, OCC_BLK, P_SIZE)
        occ_block = lax.dynamic_slice_in_dim(occ_energy, row_start, OCC_BLK, 0)
        flat_local = vir_ints.reshape(V * OCC_BLK, P_SIZE)
        energy_left = (vir_energy[:, None] - occ_block[None, :]).reshape(-1)
        block_plan = lax.dynamic_index_in_dim(roster, block_index, 0, keepdims=False)

        def pair_step(density, source):
            first_row = (source * vir_width).astype(jnp.int32)
            flat_remote = lax.dynamic_slice_in_dim(vir_ints, first_row, vir_width, 0).reshape(vir_width * OCC_BLK, P_SIZE)
            energy_block = lax.dynamic_slice_in_dim(vir_energy, first_row, vir_width, 0)
            energy_right = (energy_block[:, None] - occ_block[None, :]).reshape(-1)
            integrals = jnp.dot(flat_local, jnp.transpose(flat_remote), preferred_element_type=jnp.float32)
            amplitudes = (spin_scale * integrals / (energy_left[:, None] + energy_right[None, :])).astype(jnp.bfloat16)
            return density + jnp.dot(amplitudes, flat_remote, preferred_element_type=jnp.float32), None

        density, unused = lax.scan(pair_step, jnp.zeros((V * OCC_BLK, P_SIZE), jnp.float32), block_plan)
        return density.astype(jnp.bfloat16).reshape(V, OCC_BLK, P_SIZE)

    blocks = lax.map(one_block, jnp.arange(N_AUX, dtype=jnp.int32))
    return jnp.transpose(blocks, (1, 0, 2, 3)).reshape(V, N_AUX * OCC_BLK, P_SIZE)
```

```python
import functools

import jax
import jax.numpy as jnp
from jax import lax
from jax.experimental import pallas as pl
from jax.experimental.pallas import tpu as pltpu
from jax.sharding import PartitionSpec as P

spin_scale = 1.3
VMEM_LIMIT = 56 * 1024 * 1024


def swap(value, distance):
    count = lax.axis_size("pair")
    pairs = [(source, source ^ distance) for source in range(count)]
    return lax.ppermute(value, "pair", pairs)


def transform_kernel(width, index_ref, coeff_ref, half_ref, *out_refs):
    half = half_ref[0, 0]
    for distance, out_ref in enumerate(out_refs):
        start = pl.multiple_of((index_ref[0] ^ distance) * width, width)
        product = jnp.dot(
            coeff_ref[pl.ds(start, width), :], half, preferred_element_type=jnp.float32
        )
        out_ref[0] = product.astype(out_ref.dtype)


def transform(coeff_rows, half, orbital, pair_index):
    pair_count = lax.axis_size("pair")
    blocks, _, depth, aux_slice = half.shape
    width = coeff_rows.shape[0] // pair_count
    grid_spec = pltpu.PrefetchScalarGridSpec(
        num_scalar_prefetch=1,
        grid=(blocks,),
        in_specs=[
            pl.BlockSpec(coeff_rows.shape, lambda b, index: (0, 0)),
            pl.BlockSpec((1, 1, depth, aux_slice), lambda b, index: (b, orbital, 0, 0)),
        ],
        out_specs=[
            pl.BlockSpec((1, width, aux_slice), lambda b, index: (b, 0, 0))
        ] * pair_count,
    )
    return pl.pallas_call(
        functools.partial(transform_kernel, width),
        grid_spec=grid_spec,
        out_shape=[jax.ShapeDtypeStruct((blocks, width, aux_slice), jnp.bfloat16)] * pair_count,
        compiler_params=pltpu.CompilerParams(vmem_limit_bytes=VMEM_LIMIT),
        cost_estimate=pl.CostEstimate(
            flops=2 * blocks * coeff_rows.size * aux_slice,
            bytes_accessed=2 * (coeff_rows.size + blocks * (depth + coeff_rows.shape[0]) * aux_slice),
            transcendentals=0,
        ),
        name="transform",
    )(pair_index.reshape(1), coeff_rows, half)


def density_kernel(occ_width, remote_count, slices, has_total, *refs):
    left_energy, right_energy = refs[:2]
    local_refs = refs[2 : 2 + occ_width]
    remote_refs = refs[2 + occ_width : 2 + occ_width + remote_count]
    total_ref = refs[2 + occ_width + remote_count] if has_total else None
    out_ref, integrals, amplitudes = refs[-3:]
    step = pl.program_id(0)
    remote = jnp.concatenate([ref[0] for ref in remote_refs], axis=0)

    @pl.when(step < slices)
    def _():
        local = jnp.concatenate([ref[0] for ref in local_refs], axis=0)
        product = lax.dot_general(
            local, remote, (((1,), (1,)), ((), ())), preferred_element_type=jnp.float32
        )

        @pl.when(step == 0)
        def _():
            integrals[...] = product

        @pl.when(step > 0)
        def _():
            integrals[...] += product

        @pl.when(step == slices - 1)
        def _():
            gap = left_energy[...] + right_energy[...]
            amplitudes[...] = (spin_scale * integrals[...] / gap).astype(jnp.bfloat16)

    @pl.when(step >= slices)
    def _():
        product = jnp.dot(amplitudes[...], remote, preferred_element_type=jnp.float32)
        if has_total:
            product = product + total_ref[...]
        out_ref[...] = product.astype(out_ref.dtype)


def add_density(locals_, remotes, left_energy, right_energy, total, out_dtype):
    occ_width = len(locals_)
    slices, width, aux_slice = locals_[0].shape
    rows = occ_width * width
    columns = sum(remote.shape[1] for remote in remotes)
    in_specs = [
        pl.BlockSpec((rows, 1), lambda t: (0, 0)),
        pl.BlockSpec((1, columns), lambda t: (0, 0)),
    ]
    in_specs += [
        pl.BlockSpec((1, width, aux_slice), lambda t: (jnp.minimum(t, slices - 1), 0, 0))
    ] * occ_width
    in_specs += [
        pl.BlockSpec((1, remote.shape[1], aux_slice), lambda t: (t % slices, 0, 0))
        for remote in remotes
    ]
    out_spec = pl.BlockSpec((rows, aux_slice), lambda t: (0, jnp.maximum(t - slices, 0)))
    operands = [left_energy, right_energy, *locals_, *remotes]
    moved = 2 * slices * aux_slice * (rows + 2 * columns)
    if total is not None:
        in_specs.append(out_spec)
        operands.append(total)
        moved += total.size * 4
    out_shape = jax.ShapeDtypeStruct((rows, slices * aux_slice), out_dtype)
    moved += out_shape.size * out_shape.dtype.itemsize
    return pl.pallas_call(
        functools.partial(density_kernel, occ_width, len(remotes), slices, total is not None),
        grid=(2 * slices,),
        in_specs=in_specs,
        out_specs=out_spec,
        out_shape=out_shape,
        scratch_shapes=[
            pltpu.VMEM((rows, columns), jnp.float32),
            pltpu.VMEM((rows, columns), jnp.bfloat16),
        ],
        compiler_params=pltpu.CompilerParams(vmem_limit_bytes=VMEM_LIMIT),
        cost_estimate=pl.CostEstimate(
            flops=4 * rows * columns * slices * aux_slice,
            bytes_accessed=moved,
            transcendentals=0,
        ),
        name="density",
    )(*operands)


def per_device(half_ints, vir_coeffs, occ_energy, vir_energy, roster):
    pair_count = lax.axis_size("pair")
    aux_count = lax.axis_size("aux")
    pair_index = lax.axis_index("pair")
    aux_index = lax.axis_index("aux")
    core = pair_index % 2
    occ_rows, depth, aux_slice = half_ints.shape
    row_blocks = aux_count // pair_count
    occ_width = occ_rows // row_blocks
    step_count = roster.shape[1]

    coeff_rows = lax.all_gather(jnp.transpose(vir_coeffs), "aux", axis=0, tiled=True)
    vir_width = coeff_rows.shape[0] // pair_count
    part = vir_width // 2
    half = half_ints.reshape(row_blocks, occ_width, depth, aux_slice)

    sources = lax.dynamic_index_in_dim(roster, aux_index, 0, keepdims=False)
    occ_block = lax.dynamic_slice_in_dim(occ_energy, aux_index * occ_width, occ_width, 0)
    vir_block = lax.dynamic_slice_in_dim(vir_energy, pair_index * vir_width, vir_width, 0)
    left_energy = (vir_block[None, :] - occ_block[:, None]).reshape(-1, 1)

    locals_ = []
    for orbital in range(occ_width):
        parts = transform(coeff_rows, half, orbital, pair_index)
        gathered = jnp.zeros((aux_count, vir_width, aux_slice), jnp.bfloat16)
        for distance, piece in enumerate(parts):
            if distance:
                piece = swap(piece, distance)
            start = (pair_index ^ distance) * row_blocks
            gathered = lax.dynamic_update_slice_in_dim(gathered, piece, start, 0)
        locals_.append(lax.all_to_all(gathered, "aux", split_axis=0, concat_axis=0, tiled=True))

    total = None
    for orbital in range(occ_width):
        local = locals_[orbital]
        own = lax.dynamic_slice_in_dim(local, core * part, part, 1)
        other = lax.dynamic_slice_in_dim(local, (1 - core) * part, part, 1)
        mate = swap(other, 1)
        remotes, energies = [], []
        for position in range(step_count):
            source = sources[position]
            held = jnp.where(source == pair_index, own, mate)
            distance = 2
            while distance < pair_count:
                arrived = swap(held, distance)
                near = (source // distance) % 2 == (pair_index // distance) % 2
                held = jnp.where(near, held, arrived)
                distance *= 2
            remotes += [held, swap(held, 1)]
            for side in (core, 1 - core):
                start = source * vir_width + side * part
                energy = lax.dynamic_slice_in_dim(vir_energy, start, part, 0)
                energies.append(energy - occ_block[orbital])
        right_energy = jnp.concatenate(energies).reshape(1, -1)
        last = orbital == occ_width - 1
        total = add_density(
            locals_, remotes, left_energy, right_energy, total, jnp.bfloat16 if last else jnp.float32
        )
    aux_total = total.shape[1]
    return jnp.transpose(total.reshape(occ_width, vir_width, aux_total), (1, 0, 2))


def solution(mesh):
    in_specs = (P("pair", None, "aux"), P(None, "aux"), P(), P(), P())
    out_specs = P("pair", "aux", None)
    return jax.shard_map(
        per_device, mesh=mesh, in_specs=in_specs, out_specs=out_specs, check_vma=False
    )
```

```python
import functools

import jax
import jax.numpy as jnp
from jax import lax
from jax.experimental import pallas as pl
from jax.experimental.pallas import tpu as pltpu
from jax.sharding import PartitionSpec as P

spin_scale = 1.3
VMEM_LIMIT = 56 * 1024 * 1024
ANY = pl.BlockSpec(memory_space=pl.ANY)


def swap(value, distance, axis="pair"):
    count = lax.axis_size(axis)
    pairs = [(source, source ^ distance) for source in range(count)]
    return lax.ppermute(value, axis, pairs)


def along(value, step):
    count = lax.axis_size("aux")
    pairs = [(a, a + 2 * step) for a in range(count) if 0 <= a + 2 * step < count]
    return lax.ppermute(value, "aux", pairs)


def place_kernel(line, index_ref, *refs):
    count = 2 * line - 1
    own_refs, mate_refs, out_ref = refs[:count], refs[count:-1], refs[-1]
    here, side, core = index_ref[0], index_ref[1], index_ref[2]
    for half, piece_refs in ((core, own_refs), (1 - core, mate_refs)):
        for number, ref in enumerate(piece_refs):
            shift = (number + 1) // 2
            row = here - shift if number % 2 else here + shift

            @pl.when((row >= 0) & (row < line))
            def _():
                for slot in range(2):
                    out_ref[row, side ^ slot, half] = ref[slot]


def gather_coefficients(vir_coeffs):
    rows = jnp.transpose(vir_coeffs)
    part = rows.shape[0] // 2
    line = lax.axis_size("aux") // 2
    aux_index = lax.axis_index("aux")
    core = lax.axis_index("pair") % 2
    piece = lax.dynamic_slice_in_dim(rows, core * part, part, 0)
    both = jnp.stack([piece, swap(piece, 1, "aux")])
    own, mate = [both], [swap(both, 1)]
    below = above = both
    for _ in range(line - 1):
        below, above = along(below, 1), along(above, -1)
        own += [below, above]
        mate += [swap(below, 1), swap(above, 1)]
    depth = rows.shape[1]
    index = jnp.stack([aux_index // 2, aux_index % 2, core]).astype(jnp.int32)
    placed = pl.pallas_call(
        functools.partial(place_kernel, line),
        in_specs=[pl.BlockSpec(memory_space=pltpu.SMEM)]
        + [pl.BlockSpec(memory_space=pltpu.VMEM)] * (len(own) + len(mate)),
        out_specs=pl.BlockSpec(memory_space=pltpu.VMEM),
        out_shape=jax.ShapeDtypeStruct((line, 2, 2, part, depth), rows.dtype),
        compiler_params=pltpu.CompilerParams(vmem_limit_bytes=VMEM_LIMIT),
        cost_estimate=pl.CostEstimate(
            flops=0, bytes_accessed=4 * line * 4 * part * depth, transcendentals=0
        ),
        name="place",
    )(index, *own, *mate)
    return placed.reshape(line * 4 * part, depth)


def transform_kernel(width, index_ref, coeff_ref, half_ref, *out_refs):
    half = half_ref[0, 0]
    for distance, out_ref in enumerate(out_refs):
        start = pl.multiple_of((index_ref[0] ^ distance) * width, width)
        product = jnp.dot(
            coeff_ref[pl.ds(start, width), :], half, preferred_element_type=jnp.float32
        )
        out_ref[0] = product.astype(out_ref.dtype)


def transform(coeff_rows, half, orbital, pair_index, reach):
    blocks, _, depth, aux_slice = half.shape
    width = coeff_rows.shape[0] // lax.axis_size("pair")
    grid_spec = pltpu.PrefetchScalarGridSpec(
        num_scalar_prefetch=1,
        grid=(blocks,),
        in_specs=[
            pl.BlockSpec(coeff_rows.shape, lambda b, index: (0, 0)),
            pl.BlockSpec((1, 1, depth, aux_slice), lambda b, index: (b, orbital, 0, 0)),
        ],
        out_specs=[pl.BlockSpec((1, width, aux_slice), lambda b, index: (b, 0, 0))] * reach,
    )
    return pl.pallas_call(
        functools.partial(transform_kernel, width),
        grid_spec=grid_spec,
        out_shape=[jax.ShapeDtypeStruct((blocks, width, aux_slice), jnp.bfloat16)] * reach,
        compiler_params=pltpu.CompilerParams(vmem_limit_bytes=VMEM_LIMIT),
        cost_estimate=pl.CostEstimate(
            flops=2 * blocks * reach * width * depth * aux_slice,
            bytes_accessed=2 * (coeff_rows.size + blocks * (depth + reach * width) * aux_slice),
            transcendentals=0,
        ),
        name="transform",
    )(pair_index.reshape(1), coeff_rows, half)


def assemble_kernel(count, index_ref, *refs):
    piece_refs, out_ref = refs[:count], refs[-1]
    for number, ref in enumerate(piece_refs):
        @pl.when(pl.program_id(0) == number)
        def _():
            out_ref[...] = ref[...]


def assemble(pieces, pair_index, after):
    count = len(pieces)
    blocks, width, piece = pieces[0].shape
    whole = pl.BlockSpec((blocks, width, piece), lambda n, index: (0, 0, 0))
    return pl.pallas_call(
        functools.partial(assemble_kernel, count),
        grid_spec=pltpu.PrefetchScalarGridSpec(
            num_scalar_prefetch=1,
            grid=(count,),
            in_specs=[whole] * count + [ANY] * len(after),
            out_specs=pl.BlockSpec((blocks, width, piece), lambda n, index: (index[0] ^ n, 0, 0)),
        ),
        out_shape=jax.ShapeDtypeStruct((count * blocks, width, piece), pieces[0].dtype),
        cost_estimate=pl.CostEstimate(
            flops=0, bytes_accessed=4 * count * pieces[0].size, transcendentals=0
        ),
        name="assemble",
    )(pair_index.reshape(1), *pieces, *after)


def gate_kernel(value_ref, after_ref, out_ref):
    out_ref[...] = value_ref[...]


def gate(value, after):
    parts = 2 if value.shape[0] % 2 == 0 else 1
    spec = pl.BlockSpec((value.shape[0] // parts, *value.shape[1:]), lambda t: (t, 0, 0))
    return pl.pallas_call(
        gate_kernel,
        grid=(parts,),
        in_specs=[spec, ANY],
        out_specs=spec,
        out_shape=jax.ShapeDtypeStruct(value.shape, value.dtype),
        cost_estimate=pl.CostEstimate(flops=0, bytes_accessed=4 * value.size, transcendentals=0),
        name="gate",
    )(value, after)


GROUP = 2


def density_kernel(plan, distance_ref, *refs):
    occ_width, steps, slices, low, high, ends, segments, pair_count, starts, has_total = plan
    refs = list(refs)
    left_energy, right_energy = refs[:2]
    del refs[:2]
    local_refs = refs[:occ_width]
    del refs[:occ_width]
    held_refs = []
    for orbital in segments:
        held_refs.append([])
        for first, last in orbital:
            held_refs[-1].append((first, last, refs[:pair_count]))
            del refs[:pair_count]
    start_ref = refs.pop(0) if starts else None
    total_ref = refs.pop(0) if has_total else None
    out_ref = refs.pop(0)
    if ends:
        integrals, amplitudes, remote_ref, sems = refs
    else:
        remote_ref, sems = refs
        integrals = out_ref
    width = held_refs[0][0][2][0].shape[1]
    step = pl.program_id(0)
    turns = (high - low) // GROUP

    def copy_of(ref, first, number, t):
        return pltpu.make_async_copy(
            ref.at[t - first],
            remote_ref.at[t, pl.ds(number * width, width)],
            sems.at[number, t],
        )

    @pl.when(step == 0)
    def _():
        for orbital, parts in enumerate(held_refs):
            for first, last, blocks in parts:
                begin, end = (first, last) if ends else (max(first, low), min(last, high))

                @pl.loop(begin, end)
                def _(t):
                    for position in range(steps):
                        for distance, ref in enumerate(blocks):
                            @pl.when(distance_ref[position] == distance)
                            def _():
                                copy_of(ref, first, orbital * steps + position, t).start()

    def wait_for(t):
        for number in range(len(held_refs) * steps):
            copy_of(held_refs[0][0][2][0], t, number, t).wait()

    @pl.when(step < turns)
    def _():
        now = low + step * GROUP
        for ahead in range(GROUP):
            wait_for(now + ahead)
        local = jnp.concatenate(
            [
                jnp.concatenate([ref[ahead] for ahead in range(GROUP)], axis=1)
                for ref in local_refs
            ],
            axis=0,
        )
        remote = jnp.concatenate([remote_ref[now + ahead] for ahead in range(GROUP)], axis=1)
        product = lax.dot_general(
            local, remote, (((1,), (1,)), ((), ())), preferred_element_type=jnp.float32
        )

        @pl.when(step == 0)
        def _():
            integrals[...] = product + start_ref[...] if starts else product

        @pl.when(step > 0)
        def _():
            integrals[...] += product

        if ends:
            @pl.when(step == turns - 1)
            def _():
                gap = left_energy[...] + right_energy[...]
                amplitudes[...] = (spin_scale * integrals[...] / gap).astype(jnp.bfloat16)

    if ends:
        @pl.when(step >= turns)
        def _():
            now = step - turns

            @pl.when((now < low) | (now >= high))
            def _():
                wait_for(now)

            product = jnp.dot(amplitudes[...], remote_ref[now], preferred_element_type=jnp.float32)
            if has_total:
                product = product + total_ref[...]
            out_ref[...] = product.astype(out_ref.dtype)


def add_density(
    locals_, held, distances, left_energy, right_energy, span, ends, start=None, total=None,
    out_dtype=jnp.float32,
):
    occ_width, pair_count = len(locals_), len(held[0][0][2])
    steps = distances.shape[0]
    slices, width, aux_slice = locals_[0].shape
    rows, columns = occ_width * width, len(held) * steps * width
    low, high = span
    turns = (high - low) // GROUP
    base = low // GROUP
    in_specs = [
        pl.BlockSpec((rows, 1), lambda t, d: (0, 0)),
        pl.BlockSpec((1, columns), lambda t, d: (0, 0)),
    ]
    in_specs += [
        pl.BlockSpec(
            (GROUP, width, aux_slice), lambda t, d: (base + jnp.minimum(t, turns - 1), 0, 0)
        )
    ] * occ_width
    operands = [left_energy, right_energy, *locals_]
    for parts in held:
        for _, _, blocks in parts:
            operands += blocks
    in_specs += [ANY] * (len(operands) - len(in_specs))
    whole = pl.BlockSpec((rows, columns), lambda t, d: (0, 0))
    if start is not None:
        in_specs.append(whole)
        operands.append(start)
    moved = 2 * (high - low) * aux_slice * rows + 2 * slices * aux_slice * columns
    scratch = [
        pltpu.VMEM((slices, columns, aux_slice), jnp.bfloat16),
        pltpu.SemaphoreType.DMA((len(held) * steps, slices)),
    ]
    if ends:
        out_spec = pl.BlockSpec((rows, aux_slice), lambda t, d: (0, jnp.maximum(t - turns, 0)))
        out_shape = jax.ShapeDtypeStruct((rows, slices * aux_slice), out_dtype)
        scratch = [
            pltpu.VMEM((rows, columns), jnp.float32),
            pltpu.VMEM((rows, columns), jnp.bfloat16),
        ] + scratch
        if total is not None:
            in_specs.append(out_spec)
            operands.append(total)
            moved += total.size * 4
    else:
        out_spec = whole
        out_shape = jax.ShapeDtypeStruct((rows, columns), jnp.float32)
    moved += out_shape.size * out_shape.dtype.itemsize
    plan = (
        occ_width, steps, slices, low, high, ends,
        [[(first, last) for first, last, _ in parts] for parts in held],
        pair_count, start is not None, total is not None,
    )
    return pl.pallas_call(
        functools.partial(density_kernel, plan),
        grid_spec=pltpu.PrefetchScalarGridSpec(
            num_scalar_prefetch=1,
            grid=(turns + (slices if ends else 0),),
            in_specs=in_specs,
            out_specs=out_spec,
            scratch_shapes=scratch,
        ),
        out_shape=out_shape,
        compiler_params=pltpu.CompilerParams(vmem_limit_bytes=VMEM_LIMIT),
        cost_estimate=pl.CostEstimate(
            flops=2 * rows * columns * aux_slice * (high - low + (slices if ends else 0)),
            bytes_accessed=moved,
            transcendentals=0,
        ),
        name="density" if ends else "integrals",
    )(distances, *operands)


def per_device(half_ints, vir_coeffs, occ_energy, vir_energy, roster):
    pair_count = lax.axis_size("pair")
    aux_count = lax.axis_size("aux")
    pair_index = lax.axis_index("pair")
    aux_index = lax.axis_index("aux")
    occ_rows, depth, aux_slice = half_ints.shape
    row_blocks = aux_count // pair_count
    occ_width = occ_rows // row_blocks
    step_count = roster.shape[1]

    coeff_rows = gather_coefficients(vir_coeffs)
    vir_width = coeff_rows.shape[0] // pair_count
    half = half_ints.reshape(row_blocks, occ_width, depth, aux_slice)

    sources = lax.dynamic_index_in_dim(roster, aux_index, 0, keepdims=False)
    occ_block = lax.dynamic_slice_in_dim(occ_energy, aux_index * occ_width, occ_width, 0)
    vir_block = lax.dynamic_slice_in_dim(vir_energy, pair_index * vir_width, vir_width, 0)
    left_energy = (vir_block[None, :] - occ_block[:, None]).reshape(-1, 1)
    source_energy = [
        lax.dynamic_slice_in_dim(vir_energy, sources[position] * vir_width, vir_width, 0)
        for position in range(step_count)
    ]

    def spread(block):
        blocks = [block]
        distance = 2
        while distance < pair_count:
            blocks += [swap(b, distance) for b in blocks]
            distance *= 2
        return blocks

    def share(blocks, after=None):
        if after is not None and len(blocks) > 1:
            blocks = blocks[:-1] + [gate(blocks[-1], after)]
        return [b for block in blocks for b in (block, swap(block, 1))]

    first = []
    for raw in spread(half[:, :1]):
        own, other = transform(coeff_rows, raw, 0, pair_index, 2)
        first += [own, swap(other, 1)]
    parts = [
        transform(coeff_rows, half, orbital, pair_index, pair_count)
        for orbital in range(1, occ_width)
    ]
    moved = [first] + [
        [pieces[0]] + [swap(pieces[d], d) for d in range(1, pair_count)] for pieces in parts
    ]

    locals_, far = [], []
    middle = aux_count * 3 // 4
    for orbital in range(occ_width):
        after = [pieces[-1] for pieces in parts[1:]] if orbital == 1 else []
        if orbital > 1:
            after.append(far[orbital - 2][-1])
        if 0 < orbital < occ_width - 1:
            after += moved[orbital + 1][1:]
        sent = assemble(moved[orbital], pair_index, after)
        local = lax.all_to_all(sent, "aux", split_axis=0, concat_axis=0, tiled=True)
        locals_.append(local)
        if orbital < occ_width - 1:
            far.append(spread(local))
    halves = [spread(locals_[-1][:middle]), spread(locals_[-1][middle:])]

    distances = (sources ^ pair_index).astype(jnp.int32)

    def right_of(orbitals):
        return jnp.concatenate(
            [energy - occ_block[orbital] for orbital in orbitals for energy in source_energy]
        ).reshape(1, -1)

    total = None
    everything = (0, aux_count)
    if occ_width > 1:
        first = range(occ_width - 1)
        held = [[(0, aux_count, share(far[orbital]))] for orbital in first]
        total = add_density(
            locals_, held, distances, left_energy, right_of(first), everything, True
        )
    right_energy = right_of([occ_width - 1])
    lower = (0, middle, share(halves[0], total))
    start = add_density(
        locals_, [[lower]], distances, left_energy, right_energy, (0, middle), False
    )
    upper = (middle, aux_count, share(halves[1], start))
    total = add_density(
        locals_, [[lower, upper]], distances, left_energy, right_energy, (middle, aux_count), True,
        start=start, total=total, out_dtype=jnp.bfloat16,
    )
    return jnp.transpose(total.reshape(occ_width, vir_width, -1), (1, 0, 2))


def solution(mesh):
    in_specs = (P("pair", None, "aux"), P(None, "aux"), P(), P(), P())
    out_specs = P("pair", "aux", None)
    return jax.shard_map(
        per_device, mesh=mesh, in_specs=in_specs, out_specs=out_specs, check_vma=False
    )
```

```python
import functools

import jax
import jax.numpy as jnp
from jax import lax
from jax.experimental import pallas as pl
from jax.experimental.pallas import tpu as pltpu
from jax.sharding import PartitionSpec as P

spin_scale = 1.3
VMEM_LIMIT = 56 * 1024 * 1024
ANY = pl.BlockSpec(memory_space=pl.ANY)


def swap(value, distance, axis="pair"):
    count = lax.axis_size(axis)
    pairs = [(source, source ^ distance) for source in range(count)]
    return lax.ppermute(value, axis, pairs)


def along(value, step):
    count = lax.axis_size("aux")
    pairs = [(a, a + 2 * step) for a in range(count) if 0 <= a + 2 * step < count]
    return lax.ppermute(value, "aux", pairs)


def place_kernel(line, index_ref, *refs):
    count = 2 * line - 1
    own_refs, mate_refs, out_ref = refs[:count], refs[count:-1], refs[-1]
    here, side, core = index_ref[0], index_ref[1], index_ref[2]
    for half, piece_refs in ((core, own_refs), (1 - core, mate_refs)):
        for number, ref in enumerate(piece_refs):
            shift = (number + 1) // 2
            row = here - shift if number % 2 else here + shift

            @pl.when((row >= 0) & (row < line))
            def _():
                for slot in range(2):
                    out_ref[row, side ^ slot, half] = ref[slot]


def gather_coefficients(vir_coeffs):
    rows = jnp.transpose(vir_coeffs)
    part = rows.shape[0] // 2
    line = lax.axis_size("aux") // 2
    aux_index = lax.axis_index("aux")
    core = lax.axis_index("pair") % 2
    piece = lax.dynamic_slice_in_dim(rows, core * part, part, 0)
    both = jnp.stack([piece, swap(piece, 1, "aux")])
    own, mate = [both], [swap(both, 1)]
    below = above = both
    for _ in range(line - 1):
        below, above = along(below, 1), along(above, -1)
        own += [below, above]
        mate += [swap(below, 1), swap(above, 1)]
    depth = rows.shape[1]
    index = jnp.stack([aux_index // 2, aux_index % 2, core]).astype(jnp.int32)
    placed = pl.pallas_call(
        functools.partial(place_kernel, line),
        in_specs=[pl.BlockSpec(memory_space=pltpu.SMEM)]
        + [pl.BlockSpec(memory_space=pltpu.VMEM)] * (len(own) + len(mate)),
        out_specs=pl.BlockSpec(memory_space=pltpu.VMEM),
        out_shape=jax.ShapeDtypeStruct((line, 2, 2, part, depth), rows.dtype),
        compiler_params=pltpu.CompilerParams(vmem_limit_bytes=VMEM_LIMIT),
        cost_estimate=pl.CostEstimate(
            flops=0, bytes_accessed=4 * line * 4 * part * depth, transcendentals=0
        ),
        name="place",
    )(index, *own, *mate)
    return placed.reshape(line * 4 * part, depth)


def transform_kernel(width, distances, index_ref, coeff_ref, half_ref, *refs):
    half = half_ref[0, 0]
    out_refs = refs[-len(distances) :]
    for distance, out_ref in zip(distances, out_refs):
        place = (index_ref[0] ^ distance) % (coeff_ref.shape[0] // width)
        start = pl.multiple_of(place * width, width)
        product = jnp.dot(
            coeff_ref[pl.ds(start, width), :], half, preferred_element_type=jnp.float32
        )
        out_ref[0] = product.astype(out_ref.dtype)


def transform(coeff_rows, half, orbital, pair_index, distances, after=()):
    pair_count = lax.axis_size("pair")
    blocks, _, depth, aux_slice = half.shape
    width = coeff_rows.shape[0] // pair_count
    near = 2 if max(distances) < 2 else pair_count
    count = len(distances)
    grid_spec = pltpu.PrefetchScalarGridSpec(
        num_scalar_prefetch=1,
        grid=(blocks,),
        in_specs=[
            pl.BlockSpec((near * width, depth), lambda b, index: (index[0] // near, 0)),
            pl.BlockSpec((1, 1, depth, aux_slice), lambda b, index: (b, orbital, 0, 0)),
        ]
        + [ANY] * len(after),
        out_specs=[pl.BlockSpec((1, width, aux_slice), lambda b, index: (b, 0, 0))] * count,
    )
    return pl.pallas_call(
        functools.partial(transform_kernel, width, distances),
        grid_spec=grid_spec,
        out_shape=[jax.ShapeDtypeStruct((blocks, width, aux_slice), jnp.bfloat16)] * count,
        compiler_params=pltpu.CompilerParams(vmem_limit_bytes=VMEM_LIMIT),
        cost_estimate=pl.CostEstimate(
            flops=2 * blocks * count * width * depth * aux_slice,
            bytes_accessed=2 * (near * width * depth + blocks * (depth + count * width) * aux_slice),
            transcendentals=0,
        ),
        name="transform",
    )(pair_index.reshape(1), coeff_rows, half, *after)


def assemble_kernel(count, index_ref, *refs):
    piece_refs, (out_ref, held, arrived, left) = refs[:count], refs[-4:]
    blocks = held.shape[1]
    inward = [
        pltpu.make_async_copy(ref, held.at[number], arrived.at[number])
        for number, ref in enumerate(piece_refs)
    ]
    outward = [
        pltpu.make_async_copy(
            held.at[number],
            out_ref.at[pl.ds((index_ref[0] ^ number) * blocks, blocks)],
            left.at[number],
        )
        for number in range(count)
    ]
    for copy in inward:
        copy.start()
    for come, go in zip(inward, outward):
        come.wait()
        go.start()
    for copy in outward:
        copy.wait()


def assemble(pieces, pair_index, after):
    count = len(pieces)
    shape, dtype = pieces[0].shape, pieces[0].dtype
    return pl.pallas_call(
        functools.partial(assemble_kernel, count),
        in_specs=[pl.BlockSpec(memory_space=pltpu.SMEM)] + [ANY] * (count + len(after)),
        out_specs=ANY,
        out_shape=jax.ShapeDtypeStruct((count * shape[0], *shape[1:]), dtype),
        scratch_shapes=[
            pltpu.VMEM((count, *shape), dtype),
            pltpu.SemaphoreType.DMA((count,)),
            pltpu.SemaphoreType.DMA((count,)),
        ],
        cost_estimate=pl.CostEstimate(
            flops=0, bytes_accessed=4 * count * pieces[0].size, transcendentals=0
        ),
        name="assemble",
    )(pair_index.reshape(1), *pieces, *after)


def gate_kernel(value_ref, after_ref, out_ref):
    out_ref[...] = value_ref[...]


def gate(value, after):
    parts = 2 if value.shape[0] % 2 == 0 else 1
    spec = pl.BlockSpec((value.shape[0] // parts, *value.shape[1:]), lambda t: (t, 0, 0))
    return pl.pallas_call(
        gate_kernel,
        grid=(parts,),
        in_specs=[spec, ANY],
        out_specs=spec,
        out_shape=jax.ShapeDtypeStruct(value.shape, value.dtype),
        cost_estimate=pl.CostEstimate(flops=0, bytes_accessed=4 * value.size, transcendentals=0),
        name="gate",
    )(value, after)


GROUP = 2


def density_kernel(plan, distance_ref, *refs):
    occ_width, steps, slices, low, high, ends, segments, pair_count, starts, has_total = plan
    refs = list(refs)
    left_energy, right_energy = refs[:2]
    del refs[:2]
    local_refs = refs[:occ_width]
    del refs[:occ_width]
    held_refs = []
    for orbital in segments:
        held_refs.append([])
        for first, last in orbital:
            held_refs[-1].append((first, last, refs[:pair_count]))
            del refs[:pair_count]
    start_ref = refs.pop(0) if starts else None
    total_ref = refs.pop(0) if has_total else None
    out_ref = refs.pop(0)
    if ends:
        integrals, amplitudes, remote_ref, sems = refs
    else:
        remote_ref, sems = refs
        integrals = out_ref
    width = held_refs[0][0][2][0].shape[1]
    step = pl.program_id(0)
    turns = (high - low) // GROUP

    def copy_of(ref, first, number, t):
        return pltpu.make_async_copy(
            ref.at[t - first],
            remote_ref.at[t, pl.ds(number * width, width)],
            sems.at[number, t],
        )

    @pl.when(step == 0)
    def _():
        wanted = []
        for orbital, parts in enumerate(held_refs):
            for first, last, blocks in parts:
                wanted.append((orbital, first, blocks, max(first, low), min(last, high)))
        if ends:
            for orbital, parts in enumerate(held_refs):
                for first, last, blocks in parts:
                    wanted.append((orbital, first, blocks, first, min(last, low)))
                    wanted.append((orbital, first, blocks, max(first, high), last))
        for orbital, first, blocks, begin, end in wanted:
            if begin < end:

                @pl.loop(begin, end)
                def _(t):
                    for position in range(steps):
                        for distance, ref in enumerate(blocks):
                            @pl.when(distance_ref[position] == distance)
                            def _():
                                copy_of(ref, first, orbital * steps + position, t).start()

    def wait_for(t):
        for number in range(len(held_refs) * steps):
            copy_of(held_refs[0][0][2][0], t, number, t).wait()

    @pl.when(step < turns)
    def _():
        now = low + step * GROUP
        for ahead in range(GROUP):
            wait_for(now + ahead)
        local = jnp.concatenate(
            [
                jnp.concatenate([ref[ahead] for ahead in range(GROUP)], axis=1)
                for ref in local_refs
            ],
            axis=0,
        )
        remote = jnp.concatenate([remote_ref[now + ahead] for ahead in range(GROUP)], axis=1)
        product = lax.dot_general(
            local, remote, (((1,), (1,)), ((), ())), preferred_element_type=jnp.float32
        )

        @pl.when(step == 0)
        def _():
            integrals[...] = product + start_ref[...] if starts else product

        @pl.when(step > 0)
        def _():
            integrals[...] += product

        if ends:
            @pl.when(step == turns - 1)
            def _():
                gap = left_energy[...] + right_energy[...]
                amplitudes[...] = (spin_scale * integrals[...] / gap).astype(jnp.bfloat16)

    if ends:
        @pl.when(step >= turns)
        def _():
            now = (step - turns) * GROUP
            for ahead in range(GROUP):
                @pl.when((now + ahead < low) | (now + ahead >= high))
                def _():
                    wait_for(now + ahead)

            remote = jnp.concatenate([remote_ref[now + ahead] for ahead in range(GROUP)], axis=1)
            product = jnp.dot(amplitudes[...], remote, preferred_element_type=jnp.float32)
            if has_total:
                product = product + total_ref[...]
            out_ref[...] = product.astype(out_ref.dtype)


def add_density(
    locals_, held, distances, left_energy, right_energy, span, ends, start=None, total=None
):
    occ_width, pair_count = len(locals_), len(held[0][0][2])
    steps = distances.shape[0]
    slices, width, aux_slice = locals_[0].shape
    rows, columns = occ_width * width, len(held) * steps * width
    low, high = span
    turns = (high - low) // GROUP
    base = low // GROUP
    in_specs = [
        pl.BlockSpec((rows, 1), lambda t, d: (0, 0)),
        pl.BlockSpec((1, columns), lambda t, d: (0, 0)),
    ]
    in_specs += [
        pl.BlockSpec(
            (GROUP, width, aux_slice), lambda t, d: (base + jnp.minimum(t, turns - 1), 0, 0)
        )
    ] * occ_width
    operands = [left_energy, right_energy, *locals_]
    for parts in held:
        for _, _, blocks in parts:
            operands += blocks
    in_specs += [ANY] * (len(operands) - len(in_specs))
    whole = pl.BlockSpec((rows, columns), lambda t, d: (0, 0))
    if start is not None:
        in_specs.append(whole)
        operands.append(start)
    moved = 2 * (high - low) * aux_slice * rows + 2 * slices * aux_slice * columns
    scratch = [
        pltpu.VMEM((slices, columns, aux_slice), jnp.bfloat16),
        pltpu.SemaphoreType.DMA((len(held) * steps, slices)),
    ]
    if ends:
        out_spec = pl.BlockSpec((rows, GROUP * aux_slice), lambda t, d: (0, jnp.maximum(t - turns, 0)))
        out_shape = jax.ShapeDtypeStruct((rows, slices * aux_slice), jnp.bfloat16)
        scratch = [
            pltpu.VMEM((rows, columns), jnp.float32),
            pltpu.VMEM((rows, columns), jnp.bfloat16),
        ] + scratch
        if total is not None:
            in_specs.append(out_spec)
            operands.append(total)
            moved += total.size * 2
    else:
        out_spec = whole
        out_shape = jax.ShapeDtypeStruct((rows, columns), jnp.float32)
    moved += out_shape.size * out_shape.dtype.itemsize
    plan = (
        occ_width, steps, slices, low, high, ends,
        [[(first, last) for first, last, _ in parts] for parts in held],
        pair_count, start is not None, total is not None,
    )
    return pl.pallas_call(
        functools.partial(density_kernel, plan),
        grid_spec=pltpu.PrefetchScalarGridSpec(
            num_scalar_prefetch=1,
            grid=(turns + (slices // GROUP if ends else 0),),
            in_specs=in_specs,
            out_specs=out_spec,
            scratch_shapes=scratch,
        ),
        out_shape=out_shape,
        compiler_params=pltpu.CompilerParams(vmem_limit_bytes=VMEM_LIMIT),
        cost_estimate=pl.CostEstimate(
            flops=2 * rows * columns * aux_slice * (high - low + (slices if ends else 0)),
            bytes_accessed=moved,
            transcendentals=0,
        ),
        name="density" if ends else "integrals",
    )(distances, *operands)


def per_device(half_ints, vir_coeffs, occ_energy, vir_energy, roster):
    pair_count = lax.axis_size("pair")
    aux_count = lax.axis_size("aux")
    pair_index = lax.axis_index("pair")
    aux_index = lax.axis_index("aux")
    occ_rows, depth, aux_slice = half_ints.shape
    row_blocks = aux_count // pair_count
    occ_width = occ_rows // row_blocks
    step_count = roster.shape[1]

    coeff_rows = gather_coefficients(vir_coeffs)
    vir_width = coeff_rows.shape[0] // pair_count
    half = half_ints.reshape(row_blocks, occ_width, depth, aux_slice)

    sources = lax.dynamic_index_in_dim(roster, aux_index, 0, keepdims=False)
    occ_block = lax.dynamic_slice_in_dim(occ_energy, aux_index * occ_width, occ_width, 0)
    vir_block = lax.dynamic_slice_in_dim(vir_energy, pair_index * vir_width, vir_width, 0)
    left_energy = (vir_block[None, :] - occ_block[:, None]).reshape(-1, 1)
    source_energy = [
        lax.dynamic_slice_in_dim(vir_energy, sources[position] * vir_width, vir_width, 0)
        for position in range(step_count)
    ]

    def spread(block):
        blocks = [block]
        distance = 2
        while distance < pair_count:
            blocks += [swap(b, distance) for b in blocks]
            distance *= 2
        return blocks

    def share(blocks, after=None):
        if after is not None and len(blocks) > 1:
            blocks = blocks[:-1] + [gate(blocks[-1], after)]
        return [b for block in blocks for b in (block, swap(block, 1))]

    first = []
    for raw in spread(half[:, :1]):
        own, other = transform(coeff_rows, raw, 0, pair_index, (0, 1))
        first += [own, swap(other, 1)]
    distant = tuple(range(2, pair_count))
    parts = [
        transform(coeff_rows, half, orbital, pair_index, distant)
        for orbital in range(1, occ_width)
    ]
    moved = [first] + [[swap(piece, d) for piece, d in zip(pieces, distant)] for pieces in parts]
    for orbital in range(1, occ_width):
        own, other = transform(coeff_rows, half, orbital, pair_index, (0, 1), moved[1][:1])
        moved[orbital] = [own, swap(other, 1)] + moved[orbital]

    locals_, far = [], []
    final = occ_width - 1
    middle = aux_count * 3 // 4
    for orbital in range(occ_width):
        after = [pieces[-1] for pieces in parts[1:]] if orbital == 1 else []
        if orbital == 0 and final:
            after.append(parts[0][-1])
        if orbital > 1:
            after.append(far[orbital - 2][-1])
        if 0 < orbital < occ_width - 1:
            after += moved[orbital + 1][1:]
        sent = assemble(moved[orbital], pair_index, after)
        local = lax.all_to_all(sent, "aux", split_axis=0, concat_axis=0, tiled=True)
        locals_.append(local)
        if orbital < occ_width - 1:
            far.append(spread(local))
    halves = [spread(locals_[-1][:middle]), spread(locals_[-1][middle:])]

    distances = (sources ^ pair_index).astype(jnp.int32)

    def right_of(orbitals):
        return jnp.concatenate(
            [energy - occ_block[orbital] for orbital in orbitals for energy in source_energy]
        ).reshape(1, -1)

    total = None
    everything = (0, aux_count)
    if occ_width > 1:
        first = range(occ_width - 1)
        held = [[(0, aux_count, share(far[orbital]))] for orbital in first]
        total = add_density(
            locals_, held, distances, left_energy, right_of(first), everything, True
        )
    right_energy = right_of([occ_width - 1])
    lower = (0, middle, share(halves[0], total))
    start = add_density(
        locals_, [[lower]], distances, left_energy, right_energy, (0, middle), False
    )
    upper = (middle, aux_count, share(halves[1], start))
    total = add_density(
        locals_, [[lower, upper]], distances, left_energy, right_energy, (middle, aux_count), True,
        start=start, total=total,
    )
    return jnp.transpose(total.reshape(occ_width, vir_width, -1), (1, 0, 2))


def solution(mesh):
    in_specs = (P("pair", None, "aux"), P(None, "aux"), P(), P(), P())
    out_specs = P("pair", "aux", None)
    return jax.shard_map(
        per_device, mesh=mesh, in_specs=in_specs, out_specs=out_specs, check_vma=False
    )
```

```python
import functools

import jax
import jax.numpy as jnp
from jax import lax
from jax.experimental import pallas as pl
from jax.experimental.pallas import tpu as pltpu
from jax.sharding import PartitionSpec as P

spin_scale = 1.3
VMEM_LIMIT = 56 * 1024 * 1024
ANY = pl.BlockSpec(memory_space=pl.ANY)


def swap(value, distance, axis="pair"):
    count = lax.axis_size(axis)
    pairs = [(source, source ^ distance) for source in range(count)]
    return lax.ppermute(value, axis, pairs)


def along(value, step):
    count = lax.axis_size("aux")
    pairs = [(a, a + 2 * step) for a in range(count) if 0 <= a + 2 * step < count]
    return lax.ppermute(value, "aux", pairs)


def place_kernel(line, index_ref, *refs):
    count = 2 * line - 1
    own_refs, mate_refs, out_ref = refs[:count], refs[count:-1], refs[-1]
    here, side, core = index_ref[0], index_ref[1], index_ref[2]
    for half, piece_refs in ((core, own_refs), (1 - core, mate_refs)):
        for number, ref in enumerate(piece_refs):
            shift = (number + 1) // 2
            row = here - shift if number % 2 else here + shift

            @pl.when((row >= 0) & (row < line))
            def _():
                for slot in range(2):
                    out_ref[row, side ^ slot, half] = ref[slot]


def gather_coefficients(vir_coeffs):
    rows = jnp.transpose(vir_coeffs)
    part = rows.shape[0] // 2
    line = lax.axis_size("aux") // 2
    aux_index = lax.axis_index("aux")
    core = lax.axis_index("pair") % 2
    piece = lax.dynamic_slice_in_dim(rows, core * part, part, 0)
    both = jnp.stack([piece, swap(piece, 1, "aux")])
    own, mate = [both], [swap(both, 1)]
    below = above = both
    for _ in range(line - 1):
        below, above = along(below, 1), along(above, -1)
        own += [below, above]
        mate += [swap(below, 1), swap(above, 1)]
    depth = rows.shape[1]
    index = jnp.stack([aux_index // 2, aux_index % 2, core]).astype(jnp.int32)
    placed = pl.pallas_call(
        functools.partial(place_kernel, line),
        in_specs=[pl.BlockSpec(memory_space=pltpu.SMEM)]
        + [pl.BlockSpec(memory_space=pltpu.VMEM)] * (len(own) + len(mate)),
        out_specs=pl.BlockSpec(memory_space=pltpu.VMEM),
        out_shape=jax.ShapeDtypeStruct((line, 2, 2, part, depth), rows.dtype),
        compiler_params=pltpu.CompilerParams(vmem_limit_bytes=VMEM_LIMIT),
        cost_estimate=pl.CostEstimate(
            flops=0, bytes_accessed=4 * line * 4 * part * depth, transcendentals=0
        ),
        name="place",
    )(index, *own, *mate)
    return placed.reshape(line * 4 * part, depth)


def transform_kernel(width, distances, index_ref, coeff_ref, half_ref, *refs):
    half = half_ref[0, 0]
    out_refs = refs[-len(distances) :]
    for distance, out_ref in zip(distances, out_refs):
        place = (index_ref[0] ^ distance) % (coeff_ref.shape[0] // width)
        start = pl.multiple_of(place * width, width)
        product = jnp.dot(
            coeff_ref[pl.ds(start, width), :], half, preferred_element_type=jnp.float32
        )
        out_ref[0] = product.astype(out_ref.dtype)


def transform(coeff_rows, half, orbital, pair_index, distances, after=()):
    pair_count = lax.axis_size("pair")
    blocks, _, depth, aux_slice = half.shape
    width = coeff_rows.shape[0] // pair_count
    near = 2 if max(distances) < 2 else pair_count
    count = len(distances)
    grid_spec = pltpu.PrefetchScalarGridSpec(
        num_scalar_prefetch=1,
        grid=(blocks,),
        in_specs=[
            pl.BlockSpec((near * width, depth), lambda b, index: (index[0] // near, 0)),
            pl.BlockSpec((1, 1, depth, aux_slice), lambda b, index: (b, orbital, 0, 0)),
        ]
        + [ANY] * len(after),
        out_specs=[pl.BlockSpec((1, width, aux_slice), lambda b, index: (b, 0, 0))] * count,
    )
    return pl.pallas_call(
        functools.partial(transform_kernel, width, distances),
        grid_spec=grid_spec,
        out_shape=[jax.ShapeDtypeStruct((blocks, width, aux_slice), jnp.bfloat16)] * count,
        compiler_params=pltpu.CompilerParams(vmem_limit_bytes=VMEM_LIMIT),
        cost_estimate=pl.CostEstimate(
            flops=2 * blocks * count * width * depth * aux_slice,
            bytes_accessed=2 * (near * width * depth + blocks * (depth + count * width) * aux_slice),
            transcendentals=0,
        ),
        name="transform",
    )(pair_index.reshape(1), coeff_rows, half, *after)


def assemble_kernel(count, index_ref, *refs):
    piece_refs, (out_ref, held, arrived, left) = refs[:count], refs[-4:]
    blocks = held.shape[1]
    inward = [
        pltpu.make_async_copy(ref, held.at[number], arrived.at[number])
        for number, ref in enumerate(piece_refs)
    ]
    outward = [
        pltpu.make_async_copy(
            held.at[number],
            out_ref.at[pl.ds((index_ref[0] ^ number) * blocks, blocks)],
            left.at[number],
        )
        for number in range(count)
    ]
    for copy in inward:
        copy.start()
    for come, go in zip(inward, outward):
        come.wait()
        go.start()
    for copy in outward:
        copy.wait()


def assemble(pieces, pair_index, after):
    count = len(pieces)
    shape, dtype = pieces[0].shape, pieces[0].dtype
    return pl.pallas_call(
        functools.partial(assemble_kernel, count),
        in_specs=[pl.BlockSpec(memory_space=pltpu.SMEM)] + [ANY] * (count + len(after)),
        out_specs=ANY,
        out_shape=jax.ShapeDtypeStruct((count * shape[0], *shape[1:]), dtype),
        scratch_shapes=[
            pltpu.VMEM((count, *shape), dtype),
            pltpu.SemaphoreType.DMA((count,)),
            pltpu.SemaphoreType.DMA((count,)),
        ],
        cost_estimate=pl.CostEstimate(
            flops=0, bytes_accessed=4 * count * pieces[0].size, transcendentals=0
        ),
        name="assemble",
    )(pair_index.reshape(1), *pieces, *after)


def gate_kernel(*refs):
    del refs


def gate(value, after):
    return pl.pallas_call(
        gate_kernel,
        in_specs=[ANY] * (1 + len(after)),
        out_specs=ANY,
        out_shape=jax.ShapeDtypeStruct(value.shape, value.dtype),
        input_output_aliases={0: 0},
        cost_estimate=pl.CostEstimate(flops=0, bytes_accessed=0, transcendentals=0),
        name="gate",
    )(value, *after)


GROUP = 2


def density_kernel(plan, distance_ref, *refs):
    occ_width, steps, slices, low, high, ends, segments, pair_count, starts, has_total = plan
    refs = list(refs)
    left_energy, right_energy = refs[:2]
    del refs[:2]
    local_refs = refs[:occ_width]
    del refs[:occ_width]
    held_refs = []
    for orbital in segments:
        held_refs.append([])
        for first, last in orbital:
            held_refs[-1].append((first, last, refs[:pair_count]))
            del refs[:pair_count]
    start_ref = refs.pop(0) if starts else None
    total_ref = refs.pop(0) if has_total else None
    out_ref = refs.pop(0)
    if ends:
        integrals, amplitudes, remote_ref, sems = refs
    else:
        remote_ref, sems = refs
        integrals = out_ref
    width = held_refs[0][0][2][0].shape[1]
    step = pl.program_id(0)
    turns = (high - low) // GROUP

    def copy_of(ref, first, number, t):
        return pltpu.make_async_copy(
            ref.at[t - first],
            remote_ref.at[t, pl.ds(number * width, width)],
            sems.at[number, t],
        )

    @pl.when(step == 0)
    def _():
        wanted = []
        for orbital, parts in enumerate(held_refs):
            for first, last, blocks in parts:
                wanted.append((orbital, first, blocks, max(first, low), min(last, high)))
        if ends:
            for orbital, parts in enumerate(held_refs):
                for first, last, blocks in parts:
                    wanted.append((orbital, first, blocks, first, min(last, low)))
                    wanted.append((orbital, first, blocks, max(first, high), last))
        for orbital, first, blocks, begin, end in wanted:
            if begin < end:

                @pl.loop(begin, end)
                def _(t):
                    for position in range(steps):
                        for distance, ref in enumerate(blocks):
                            @pl.when(distance_ref[position] == distance)
                            def _():
                                copy_of(ref, first, orbital * steps + position, t).start()

    def wait_for(t):
        for number in range(len(held_refs) * steps):
            copy_of(held_refs[0][0][2][0], t, number, t).wait()

    @pl.when(step < turns)
    def _():
        now = low + step * GROUP
        for ahead in range(GROUP):
            wait_for(now + ahead)
        local = jnp.concatenate(
            [
                jnp.concatenate([ref[ahead] for ahead in range(GROUP)], axis=1)
                for ref in local_refs
            ],
            axis=0,
        )
        remote = jnp.concatenate([remote_ref[now + ahead] for ahead in range(GROUP)], axis=1)
        product = lax.dot_general(
            local, remote, (((1,), (1,)), ((), ())), preferred_element_type=jnp.float32
        )

        @pl.when(step == 0)
        def _():
            integrals[...] = product + start_ref[...] if starts else product

        @pl.when(step > 0)
        def _():
            integrals[...] += product

        if ends:
            @pl.when(step == turns - 1)
            def _():
                gap = left_energy[...] + right_energy[...]
                amplitudes[...] = (spin_scale * integrals[...] / gap).astype(jnp.bfloat16)

    if ends:
        @pl.when(step >= turns)
        def _():
            now = (step - turns) * GROUP
            for ahead in range(GROUP):
                @pl.when((now + ahead < low) | (now + ahead >= high))
                def _():
                    wait_for(now + ahead)

            remote = jnp.concatenate([remote_ref[now + ahead] for ahead in range(GROUP)], axis=1)
            product = jnp.dot(amplitudes[...], remote, preferred_element_type=jnp.float32)
            if has_total:
                product = product + total_ref[...]
            out_ref[...] = product.astype(out_ref.dtype)


def add_density(
    locals_, held, distances, left_energy, right_energy, span, ends, start=None, total=None
):
    occ_width, pair_count = len(locals_), len(held[0][0][2])
    steps = distances.shape[0]
    slices, width, aux_slice = locals_[0].shape
    rows, columns = occ_width * width, len(held) * steps * width
    low, high = span
    turns = (high - low) // GROUP
    base = low // GROUP
    in_specs = [
        pl.BlockSpec((rows, 1), lambda t, d: (0, 0)),
        pl.BlockSpec((1, columns), lambda t, d: (0, 0)),
    ]
    in_specs += [
        pl.BlockSpec(
            (GROUP, width, aux_slice), lambda t, d: (base + jnp.minimum(t, turns - 1), 0, 0)
        )
    ] * occ_width
    operands = [left_energy, right_energy, *locals_]
    for parts in held:
        for _, _, blocks in parts:
            operands += blocks
    in_specs += [ANY] * (len(operands) - len(in_specs))
    whole = pl.BlockSpec((rows, columns), lambda t, d: (0, 0))
    if start is not None:
        in_specs.append(whole)
        operands.append(start)
    moved = 2 * (high - low) * aux_slice * rows + 2 * slices * aux_slice * columns
    scratch = [
        pltpu.VMEM((slices, columns, aux_slice), jnp.bfloat16),
        pltpu.SemaphoreType.DMA((len(held) * steps, slices)),
    ]
    if ends:
        out_spec = pl.BlockSpec((rows, GROUP * aux_slice), lambda t, d: (0, jnp.maximum(t - turns, 0)))
        out_shape = jax.ShapeDtypeStruct((rows, slices * aux_slice), jnp.bfloat16)
        scratch = [
            pltpu.VMEM((rows, columns), jnp.float32),
            pltpu.VMEM((rows, columns), jnp.bfloat16),
        ] + scratch
        if total is not None:
            in_specs.append(out_spec)
            operands.append(total)
            moved += total.size * 2
    else:
        out_spec = whole
        out_shape = jax.ShapeDtypeStruct((rows, columns), jnp.float32)
    moved += out_shape.size * out_shape.dtype.itemsize
    plan = (
        occ_width, steps, slices, low, high, ends,
        [[(first, last) for first, last, _ in parts] for parts in held],
        pair_count, start is not None, total is not None,
    )
    return pl.pallas_call(
        functools.partial(density_kernel, plan),
        grid_spec=pltpu.PrefetchScalarGridSpec(
            num_scalar_prefetch=1,
            grid=(turns + (slices // GROUP if ends else 0),),
            in_specs=in_specs,
            out_specs=out_spec,
            scratch_shapes=scratch,
        ),
        out_shape=out_shape,
        compiler_params=pltpu.CompilerParams(vmem_limit_bytes=VMEM_LIMIT),
        cost_estimate=pl.CostEstimate(
            flops=2 * rows * columns * aux_slice * (high - low + (slices if ends else 0)),
            bytes_accessed=moved,
            transcendentals=0,
        ),
        name="density" if ends else "integrals",
    )(distances, *operands)


def per_device(half_ints, vir_coeffs, occ_energy, vir_energy, roster):
    pair_count = lax.axis_size("pair")
    aux_count = lax.axis_size("aux")
    pair_index = lax.axis_index("pair")
    aux_index = lax.axis_index("aux")
    occ_rows, depth, aux_slice = half_ints.shape
    row_blocks = aux_count // pair_count
    occ_width = occ_rows // row_blocks
    step_count = roster.shape[1]

    coeff_rows = gather_coefficients(vir_coeffs)
    vir_width = coeff_rows.shape[0] // pair_count
    half = half_ints.reshape(row_blocks, occ_width, depth, aux_slice)

    sources = lax.dynamic_index_in_dim(roster, aux_index, 0, keepdims=False)
    occ_block = lax.dynamic_slice_in_dim(occ_energy, aux_index * occ_width, occ_width, 0)
    vir_block = lax.dynamic_slice_in_dim(vir_energy, pair_index * vir_width, vir_width, 0)
    left_energy = (vir_block[None, :] - occ_block[:, None]).reshape(-1, 1)
    source_energy = [
        lax.dynamic_slice_in_dim(vir_energy, sources[position] * vir_width, vir_width, 0)
        for position in range(step_count)
    ]

    def spread(block):
        blocks = [block]
        distance = 2
        while distance < pair_count:
            blocks += [swap(b, distance) for b in blocks]
            distance *= 2
        return blocks

    def share(blocks, after=None):
        if after is not None and len(blocks) > 1:
            blocks = blocks[:-1] + [gate(blocks[-1], [after])]
        return [b for block in blocks for b in (block, swap(block, 1))]

    first = []
    for raw in spread(half[:, :1]):
        own, other = transform(coeff_rows, raw, 0, pair_index, (0, 1))
        first += [own, swap(other, 1)]
    distant = tuple(range(2, pair_count))
    parts = [
        transform(coeff_rows, half, orbital, pair_index, distant)
        for orbital in range(1, occ_width)
    ]
    moved = [first] + [[swap(piece, d) for piece, d in zip(pieces, distant)] for pieces in parts]
    for orbital in range(1, occ_width):
        own, other = transform(coeff_rows, half, orbital, pair_index, (0, 1), moved[1][:1])
        moved[orbital] = [own, swap(other, 1)] + moved[orbital]

    locals_, far = [], []
    final = occ_width - 1
    middle = aux_count * 3 // 4
    for orbital in range(occ_width):
        early = [parts[0][-1]] if orbital == 0 and final else []
        sent = assemble(moved[orbital], pair_index, early)
        after = []
        if 0 < orbital < final:
            after += moved[orbital + 1][1:]
        if orbital > 1:
            after.append(far[orbital - 2][-1])
        if after:
            sent = gate(sent, after)
        local = lax.all_to_all(sent, "aux", split_axis=0, concat_axis=0, tiled=True)
        locals_.append(local)
        if orbital < occ_width - 1:
            far.append(spread(local))
    halves = [spread(locals_[-1][:middle]), spread(locals_[-1][middle:])]

    distances = (sources ^ pair_index).astype(jnp.int32)

    def right_of(orbitals):
        return jnp.concatenate(
            [energy - occ_block[orbital] for orbital in orbitals for energy in source_energy]
        ).reshape(1, -1)

    total = None
    everything = (0, aux_count)
    if occ_width > 1:
        first = range(occ_width - 1)
        held = [[(0, aux_count, share(far[orbital]))] for orbital in first]
        total = add_density(
            locals_, held, distances, left_energy, right_of(first), everything, True
        )
    right_energy = right_of([occ_width - 1])
    lower = (0, middle, share(halves[0], total))
    start = add_density(
        locals_, [[lower]], distances, left_energy, right_energy, (0, middle), False
    )
    upper = (middle, aux_count, share(halves[1], start))
    total = add_density(
        locals_, [[lower, upper]], distances, left_energy, right_energy, (middle, aux_count), True,
        start=start, total=total,
    )
    return jnp.transpose(total.reshape(occ_width, vir_width, -1), (1, 0, 2))


def solution(mesh):
    in_specs = (P("pair", None, "aux"), P(None, "aux"), P(), P(), P())
    out_specs = P("pair", "aux", None)
    return jax.shard_map(
        per_device, mesh=mesh, in_specs=in_specs, out_specs=out_specs, check_vma=False
    )
```

```python
import functools

import jax
import jax.numpy as jnp
from jax import lax
from jax.experimental import pallas as pl
from jax.experimental.pallas import tpu as pltpu
from jax.sharding import PartitionSpec as P

spin_scale = 1.3
VMEM_LIMIT = 56 * 1024 * 1024
ANY = pl.BlockSpec(memory_space=pl.ANY)


def swap(value, distance, axis="pair"):
    count = lax.axis_size(axis)
    pairs = [(source, source ^ distance) for source in range(count)]
    return lax.ppermute(value, axis, pairs)


def along(value, step):
    count = lax.axis_size("aux")
    pairs = [(a, a + 2 * step) for a in range(count) if 0 <= a + 2 * step < count]
    return lax.ppermute(value, "aux", pairs)


def place_kernel(line, index_ref, *refs):
    count = 2 * line - 1
    own_refs, mate_refs, out_ref = refs[:count], refs[count:-1], refs[-1]
    here, side, core = index_ref[0], index_ref[1], index_ref[2]
    for half, piece_refs in ((core, own_refs), (1 - core, mate_refs)):
        for number, ref in enumerate(piece_refs):
            shift = (number + 1) // 2
            row = here - shift if number % 2 else here + shift

            @pl.when((row >= 0) & (row < line))
            def _():
                for slot in range(2):
                    out_ref[row, side ^ slot, half] = ref[slot]


def gather_coefficients(vir_coeffs):
    rows = jnp.transpose(vir_coeffs)
    part = rows.shape[0] // 2
    line = lax.axis_size("aux") // 2
    aux_index = lax.axis_index("aux")
    core = lax.axis_index("pair") % 2
    piece = lax.dynamic_slice_in_dim(rows, core * part, part, 0)
    both = jnp.stack([piece, swap(piece, 1, "aux")])
    own, mate = [both], [swap(both, 1)]
    below = above = both
    for _ in range(line - 1):
        below, above = along(below, 1), along(above, -1)
        own += [below, above]
        mate += [swap(below, 1), swap(above, 1)]
    depth = rows.shape[1]
    index = jnp.stack([aux_index // 2, aux_index % 2, core]).astype(jnp.int32)
    placed = pl.pallas_call(
        functools.partial(place_kernel, line),
        in_specs=[pl.BlockSpec(memory_space=pltpu.SMEM)]
        + [pl.BlockSpec(memory_space=pltpu.VMEM)] * (len(own) + len(mate)),
        out_specs=pl.BlockSpec(memory_space=pltpu.VMEM),
        out_shape=jax.ShapeDtypeStruct((line, 2, 2, part, depth), rows.dtype),
        compiler_params=pltpu.CompilerParams(vmem_limit_bytes=VMEM_LIMIT),
        cost_estimate=pl.CostEstimate(
            flops=0, bytes_accessed=4 * line * 4 * part * depth, transcendentals=0
        ),
        name="place",
    )(index, *own, *mate)
    return placed.reshape(line * 4 * part, depth)


def transform_kernel(width, distances, index_ref, coeff_ref, half_ref, *refs):
    half = half_ref[0, 0]
    out_refs = refs[-len(distances) :]
    for distance, out_ref in zip(distances, out_refs):
        place = (index_ref[0] ^ distance) % (coeff_ref.shape[0] // width)
        start = pl.multiple_of(place * width, width)
        product = jnp.dot(
            coeff_ref[pl.ds(start, width), :], half, preferred_element_type=jnp.float32
        )
        out_ref[0] = product.astype(out_ref.dtype)


def transform(coeff_rows, half, orbital, pair_index, distances, after=()):
    pair_count = lax.axis_size("pair")
    blocks, _, depth, aux_slice = half.shape
    width = coeff_rows.shape[0] // pair_count
    near = 2 if max(distances) < 2 else pair_count
    count = len(distances)
    grid_spec = pltpu.PrefetchScalarGridSpec(
        num_scalar_prefetch=1,
        grid=(blocks,),
        in_specs=[
            pl.BlockSpec((near * width, depth), lambda b, index: (index[0] // near, 0)),
            pl.BlockSpec((1, 1, depth, aux_slice), lambda b, index: (b, orbital, 0, 0)),
        ]
        + [ANY] * len(after),
        out_specs=[pl.BlockSpec((1, width, aux_slice), lambda b, index: (b, 0, 0))] * count,
    )
    return pl.pallas_call(
        functools.partial(transform_kernel, width, distances),
        grid_spec=grid_spec,
        out_shape=[jax.ShapeDtypeStruct((blocks, width, aux_slice), jnp.bfloat16)] * count,
        compiler_params=pltpu.CompilerParams(vmem_limit_bytes=VMEM_LIMIT),
        cost_estimate=pl.CostEstimate(
            flops=2 * blocks * count * width * depth * aux_slice,
            bytes_accessed=2 * (near * width * depth + blocks * (depth + count * width) * aux_slice),
            transcendentals=0,
        ),
        name="transform",
    )(pair_index.reshape(1), coeff_rows, half, *after)


def assemble_kernel(count, index_ref, *refs):
    piece_refs, (out_ref, held, arrived, left) = refs[:count], refs[-4:]
    blocks = held.shape[1]
    inward = [
        pltpu.make_async_copy(ref, held.at[number], arrived.at[number])
        for number, ref in enumerate(piece_refs)
    ]
    outward = [
        pltpu.make_async_copy(
            held.at[number],
            out_ref.at[pl.ds((index_ref[0] ^ number) * blocks, blocks)],
            left.at[number],
        )
        for number in range(count)
    ]
    for copy in inward:
        copy.start()
    for come, go in zip(inward, outward):
        come.wait()
        go.start()
    for copy in outward:
        copy.wait()


def assemble(pieces, pair_index, after):
    count = len(pieces)
    shape, dtype = pieces[0].shape, pieces[0].dtype
    return pl.pallas_call(
        functools.partial(assemble_kernel, count),
        in_specs=[pl.BlockSpec(memory_space=pltpu.SMEM)] + [ANY] * (count + len(after)),
        out_specs=ANY,
        out_shape=jax.ShapeDtypeStruct((count * shape[0], *shape[1:]), dtype),
        scratch_shapes=[
            pltpu.VMEM((count, *shape), dtype),
            pltpu.SemaphoreType.DMA((count,)),
            pltpu.SemaphoreType.DMA((count,)),
        ],
        cost_estimate=pl.CostEstimate(
            flops=0, bytes_accessed=4 * count * pieces[0].size, transcendentals=0
        ),
        name="assemble",
    )(pair_index.reshape(1), *pieces, *after)


def gate_kernel(*refs):
    del refs


def gate(value, after):
    return pl.pallas_call(
        gate_kernel,
        in_specs=[ANY] * (1 + len(after)),
        out_specs=ANY,
        out_shape=jax.ShapeDtypeStruct(value.shape, value.dtype),
        input_output_aliases={0: 0},
        cost_estimate=pl.CostEstimate(flops=0, bytes_accessed=0, transcendentals=0),
        name="gate",
    )(value, *after)


GROUP = 2


def density_kernel(plan, distance_ref, *refs):
    occ_width, steps, slices, low, high, ends, segments, pair_count, starts, has_total = plan
    refs = list(refs)
    left_energy, right_energy = refs[:2]
    del refs[:2]
    local_refs = refs[:occ_width]
    del refs[:occ_width]
    held_refs = []
    for orbital in segments:
        held_refs.append([])
        for first, last in orbital:
            held_refs[-1].append((first, last, refs[:pair_count]))
            del refs[:pair_count]
    start_ref = refs.pop(0) if starts else None
    total_ref = refs.pop(0) if has_total else None
    out_ref = refs.pop(0)
    if starts:
        start_buffer, start_sem = refs[-2:]
        del refs[-2:]
    if ends:
        integrals, amplitudes, remote_ref, sems = refs
    else:
        remote_ref, sems = refs
        integrals = out_ref
    width = held_refs[0][0][2][0].shape[1]
    step = pl.program_id(0)
    turns = (high - low) // GROUP

    def copy_of(ref, first, number, t):
        return pltpu.make_async_copy(
            ref.at[t - first],
            remote_ref.at[t, pl.ds(number * width, width)],
            sems.at[number, t],
        )

    @pl.when(step == 0)
    def _():
        wanted = []
        for orbital, parts in enumerate(held_refs):
            for first, last, blocks in parts:
                wanted.append((orbital, first, blocks, max(first, low), min(last, high)))
        if ends:
            for orbital, parts in enumerate(held_refs):
                for first, last, blocks in parts:
                    wanted.append((orbital, first, blocks, first, min(last, low)))
                    wanted.append((orbital, first, blocks, max(first, high), last))
        for orbital, first, blocks, begin, end in wanted:
            if begin < end:

                @pl.loop(begin, end)
                def _(t):
                    for position in range(steps):
                        for distance, ref in enumerate(blocks):
                            @pl.when(distance_ref[position] == distance)
                            def _():
                                copy_of(ref, first, orbital * steps + position, t).start()

    if starts:
        @pl.when(step == 0)
        def _():
            pltpu.make_async_copy(start_ref, start_buffer, start_sem).start()

    def wait_for(t):
        for number in range(len(held_refs) * steps):
            copy_of(held_refs[0][0][2][0], t, number, t).wait()

    @pl.when(step < turns)
    def _():
        now = low + step * GROUP
        for ahead in range(GROUP):
            wait_for(now + ahead)
        local = jnp.concatenate(
            [
                jnp.concatenate([ref[ahead] for ahead in range(GROUP)], axis=1)
                for ref in local_refs
            ],
            axis=0,
        )
        remote = jnp.concatenate([remote_ref[now + ahead] for ahead in range(GROUP)], axis=1)
        product = lax.dot_general(
            local, remote, (((1,), (1,)), ((), ())), preferred_element_type=jnp.float32
        )

        @pl.when(step == 0)
        def _():
            if starts:
                pltpu.make_async_copy(start_ref, start_buffer, start_sem).wait()
                integrals[...] = product + start_buffer[...]
            else:
                integrals[...] = product

        @pl.when(step > 0)
        def _():
            integrals[...] += product

        if ends:
            @pl.when(step == turns - 1)
            def _():
                gap = left_energy[...] + right_energy[...]
                amplitudes[...] = (spin_scale * integrals[...] / gap).astype(jnp.bfloat16)

    if ends:
        @pl.when(step >= turns)
        def _():
            now = (step - turns) * GROUP
            for ahead in range(GROUP):
                @pl.when((now + ahead < low) | (now + ahead >= high))
                def _():
                    wait_for(now + ahead)

            remote = jnp.concatenate([remote_ref[now + ahead] for ahead in range(GROUP)], axis=1)
            product = jnp.dot(amplitudes[...], remote, preferred_element_type=jnp.float32)
            if has_total:
                product = product + total_ref[...]
            out_ref[...] = product.astype(out_ref.dtype)


def add_density(
    locals_, held, distances, left_energy, right_energy, span, ends, start=None, total=None
):
    occ_width, pair_count = len(locals_), len(held[0][0][2])
    steps = distances.shape[0]
    slices, width, aux_slice = locals_[0].shape
    rows, columns = occ_width * width, len(held) * steps * width
    low, high = span
    turns = (high - low) // GROUP
    base = low // GROUP
    in_specs = [
        pl.BlockSpec((rows, 1), lambda t, d: (0, 0)),
        pl.BlockSpec((1, columns), lambda t, d: (0, 0)),
    ]
    in_specs += [
        pl.BlockSpec(
            (GROUP, width, aux_slice), lambda t, d: (base + jnp.minimum(t, turns - 1), 0, 0)
        )
    ] * occ_width
    operands = [left_energy, right_energy, *locals_]
    for parts in held:
        for _, _, blocks in parts:
            operands += blocks
    in_specs += [ANY] * (len(operands) - len(in_specs))
    whole = pl.BlockSpec((rows, columns), lambda t, d: (0, 0))
    if start is not None:
        in_specs.append(ANY)
        operands.append(start)
    moved = 2 * (high - low) * aux_slice * rows + 2 * slices * aux_slice * columns
    scratch = [
        pltpu.VMEM((slices, columns, aux_slice), jnp.bfloat16),
        pltpu.SemaphoreType.DMA((len(held) * steps, slices)),
    ]
    if ends:
        out_spec = pl.BlockSpec((rows, GROUP * aux_slice), lambda t, d: (0, jnp.maximum(t - turns, 0)))
        out_shape = jax.ShapeDtypeStruct((rows, slices * aux_slice), jnp.bfloat16)
        scratch = [
            pltpu.VMEM((rows, columns), jnp.float32),
            pltpu.VMEM((rows, columns), jnp.bfloat16),
        ] + scratch
        if total is not None:
            in_specs.append(out_spec)
            operands.append(total)
            moved += total.size * 2
    else:
        out_spec = whole
        out_shape = jax.ShapeDtypeStruct((rows, columns), jnp.float32)
    moved += out_shape.size * out_shape.dtype.itemsize
    if start is not None:
        scratch += [pltpu.VMEM((rows, columns), jnp.float32), pltpu.SemaphoreType.DMA]
    plan = (
        occ_width, steps, slices, low, high, ends,
        [[(first, last) for first, last, _ in parts] for parts in held],
        pair_count, start is not None, total is not None,
    )
    return pl.pallas_call(
        functools.partial(density_kernel, plan),
        grid_spec=pltpu.PrefetchScalarGridSpec(
            num_scalar_prefetch=1,
            grid=(turns + (slices // GROUP if ends else 0),),
            in_specs=in_specs,
            out_specs=out_spec,
            scratch_shapes=scratch,
        ),
        out_shape=out_shape,
        compiler_params=pltpu.CompilerParams(vmem_limit_bytes=VMEM_LIMIT),
        cost_estimate=pl.CostEstimate(
            flops=2 * rows * columns * aux_slice * (high - low + (slices if ends else 0)),
            bytes_accessed=moved,
            transcendentals=0,
        ),
        name="density" if ends else "integrals",
    )(distances, *operands)


def per_device(half_ints, vir_coeffs, occ_energy, vir_energy, roster):
    pair_count = lax.axis_size("pair")
    aux_count = lax.axis_size("aux")
    pair_index = lax.axis_index("pair")
    aux_index = lax.axis_index("aux")
    occ_rows, depth, aux_slice = half_ints.shape
    row_blocks = aux_count // pair_count
    occ_width = occ_rows // row_blocks
    step_count = roster.shape[1]

    coeff_rows = gather_coefficients(vir_coeffs)
    vir_width = coeff_rows.shape[0] // pair_count
    half = half_ints.reshape(row_blocks, occ_width, depth, aux_slice)

    sources = lax.dynamic_index_in_dim(roster, aux_index, 0, keepdims=False)
    occ_block = lax.dynamic_slice_in_dim(occ_energy, aux_index * occ_width, occ_width, 0)
    vir_block = lax.dynamic_slice_in_dim(vir_energy, pair_index * vir_width, vir_width, 0)
    left_energy = (vir_block[None, :] - occ_block[:, None]).reshape(-1, 1)
    source_energy = [
        lax.dynamic_slice_in_dim(vir_energy, sources[position] * vir_width, vir_width, 0)
        for position in range(step_count)
    ]

    def spread(block):
        blocks = [block]
        distance = 2
        while distance < pair_count:
            blocks += [swap(b, distance) for b in blocks]
            distance *= 2
        return blocks

    def share(blocks, after=None):
        if after is not None and len(blocks) > 1:
            blocks = blocks[:-1] + [gate(blocks[-1], after)]
        return [b for block in blocks for b in (block, swap(block, 1))]

    distant = tuple(range(2, pair_count))
    parts = [
        transform(coeff_rows, half, orbital, pair_index, distant)
        for orbital in range(1, occ_width)
    ]
    first = []
    for raw in spread(half[:, :1]):
        before = [] if first or not parts else [parts[0][-1]]
        own, other = transform(coeff_rows, raw, 0, pair_index, (0, 1), before)
        first += [own, swap(other, 1)]
    moved = [first] + [[swap(piece, d) for piece, d in zip(pieces, distant)] for pieces in parts]
    for orbital in range(1, occ_width):
        own, other = transform(coeff_rows, half, orbital, pair_index, (0, 1), moved[1][:1])
        moved[orbital] = [own, swap(other, 1)] + moved[orbital]

    locals_, far = [], []
    final = occ_width - 1
    middle = aux_count * 3 // 4
    for orbital in range(occ_width):
        sent = assemble(moved[orbital], pair_index, [])
        after = []
        if 0 < orbital < final:
            after += moved[orbital + 1][1:]
        if orbital > 1:
            after.append(far[orbital - 2][-1])
        if after:
            sent = gate(sent, after)
        local = lax.all_to_all(sent, "aux", split_axis=0, concat_axis=0, tiled=True)
        locals_.append(local)
        if orbital < occ_width - 1:
            far.append(spread(local))
    upper_rows = locals_[-1][middle:]
    halves = [spread(locals_[-1][:middle]), spread(upper_rows)]

    distances = (sources ^ pair_index).astype(jnp.int32)

    def right_of(orbitals):
        return jnp.concatenate(
            [energy - occ_block[orbital] for orbital in orbitals for energy in source_energy]
        ).reshape(1, -1)

    total = None
    everything = (0, aux_count)
    if occ_width > 1:
        first = range(occ_width - 1)
        held = [[(0, aux_count, share(far[orbital]))] for orbital in first]
        total = add_density(
            locals_, held, distances, left_energy, right_of(first), everything, True
        )
    right_energy = right_of([occ_width - 1])
    lower = (0, middle, share(halves[0], [upper_rows] if total is None else [total, upper_rows]))
    start = add_density(
        locals_, [[lower]], distances, left_energy, right_energy, (0, middle), False
    )
    upper = (middle, aux_count, share(halves[1], [start]))
    total = add_density(
        locals_, [[lower, upper]], distances, left_energy, right_energy, (middle, aux_count), True,
        start=start, total=total,
    )
    return jnp.transpose(total.reshape(occ_width, vir_width, -1), (1, 0, 2))


def solution(mesh):
    in_specs = (P("pair", None, "aux"), P(None, "aux"), P(), P(), P())
    out_specs = P("pair", "aux", None)
    return jax.shard_map(
        per_device, mesh=mesh, in_specs=in_specs, out_specs=out_specs, check_vma=False
    )
```

```python
import functools

import jax
import jax.numpy as jnp
from jax import lax
from jax.experimental import pallas as pl
from jax.experimental.pallas import tpu as pltpu
from jax.sharding import PartitionSpec as P

spin_scale = 1.3
VMEM_LIMIT = 56 * 1024 * 1024
ANY = pl.BlockSpec(memory_space=pl.ANY)


def swap(value, distance, axis="pair"):
    count = lax.axis_size(axis)
    pairs = [(source, source ^ distance) for source in range(count)]
    return lax.ppermute(value, axis, pairs)


def along(value, step):
    count = lax.axis_size("aux")
    pairs = [(a, a + 2 * step) for a in range(count) if 0 <= a + 2 * step < count]
    return lax.ppermute(value, "aux", pairs)


def place_kernel(line, index_ref, *refs):
    count = 2 * line - 1
    own_refs, mate_refs, out_ref = refs[:count], refs[count:-1], refs[-1]
    here, side, core = index_ref[0], index_ref[1], index_ref[2]
    for half, piece_refs in ((core, own_refs), (1 - core, mate_refs)):
        for number, ref in enumerate(piece_refs):
            shift = (number + 1) // 2
            row = here - shift if number % 2 else here + shift

            @pl.when((row >= 0) & (row < line))
            def _():
                for slot in range(2):
                    out_ref[row, side ^ slot, half] = ref[slot]


def gather_coefficients(vir_coeffs):
    rows = jnp.transpose(vir_coeffs)
    part = rows.shape[0] // 2
    line = lax.axis_size("aux") // 2
    aux_index = lax.axis_index("aux")
    core = lax.axis_index("pair") % 2
    piece = lax.dynamic_slice_in_dim(rows, core * part, part, 0)
    both = jnp.stack([piece, swap(piece, 1, "aux")])
    own, mate = [both], [swap(both, 1)]
    below = above = both
    for _ in range(line - 1):
        below, above = along(below, 1), along(above, -1)
        own += [below, above]
        mate += [swap(below, 1), swap(above, 1)]
    depth = rows.shape[1]
    index = jnp.stack([aux_index // 2, aux_index % 2, core]).astype(jnp.int32)
    placed = pl.pallas_call(
        functools.partial(place_kernel, line),
        in_specs=[pl.BlockSpec(memory_space=pltpu.SMEM)]
        + [pl.BlockSpec(memory_space=pltpu.VMEM)] * (len(own) + len(mate)),
        out_specs=pl.BlockSpec(memory_space=pltpu.VMEM),
        out_shape=jax.ShapeDtypeStruct((line, 2, 2, part, depth), rows.dtype),
        compiler_params=pltpu.CompilerParams(vmem_limit_bytes=VMEM_LIMIT),
        cost_estimate=pl.CostEstimate(
            flops=0, bytes_accessed=4 * line * 4 * part * depth, transcendentals=0
        ),
        name="place",
    )(index, *own, *mate)
    return placed.reshape(line * 4 * part, depth)


def transform_kernel(width, distances, index_ref, coeff_ref, half_ref, *refs):
    half = half_ref[0, 0]
    out_refs = refs[-len(distances) :]
    for distance, out_ref in zip(distances, out_refs):
        place = (index_ref[0] ^ distance) % (coeff_ref.shape[0] // width)
        start = pl.multiple_of(place * width, width)
        product = jnp.dot(
            coeff_ref[pl.ds(start, width), :], half, preferred_element_type=jnp.float32
        )
        out_ref[0] = product.astype(out_ref.dtype)


def transform(coeff_rows, half, orbital, pair_index, distances, after=()):
    pair_count = lax.axis_size("pair")
    blocks, _, depth, aux_slice = half.shape
    width = coeff_rows.shape[0] // pair_count
    near = 2 if max(distances) < 2 else pair_count
    count = len(distances)
    grid_spec = pltpu.PrefetchScalarGridSpec(
        num_scalar_prefetch=1,
        grid=(blocks,),
        in_specs=[
            pl.BlockSpec((near * width, depth), lambda b, index: (index[0] // near, 0)),
            pl.BlockSpec((1, 1, depth, aux_slice), lambda b, index: (b, orbital, 0, 0)),
        ]
        + [ANY] * len(after),
        out_specs=[pl.BlockSpec((1, width, aux_slice), lambda b, index: (b, 0, 0))] * count,
    )
    return pl.pallas_call(
        functools.partial(transform_kernel, width, distances),
        grid_spec=grid_spec,
        out_shape=[jax.ShapeDtypeStruct((blocks, width, aux_slice), jnp.bfloat16)] * count,
        compiler_params=pltpu.CompilerParams(vmem_limit_bytes=VMEM_LIMIT),
        cost_estimate=pl.CostEstimate(
            flops=2 * blocks * count * width * depth * aux_slice,
            bytes_accessed=2 * (near * width * depth + blocks * (depth + count * width) * aux_slice),
            transcendentals=0,
        ),
        name="transform",
    )(pair_index.reshape(1), coeff_rows, half, *after)


def assemble_kernel(count, index_ref, *refs):
    piece_refs, (out_ref, held, arrived, left) = refs[:count], refs[-4:]
    blocks = held.shape[1]
    inward = [
        pltpu.make_async_copy(ref, held.at[number], arrived.at[number])
        for number, ref in enumerate(piece_refs)
    ]
    outward = [
        pltpu.make_async_copy(
            held.at[number],
            out_ref.at[pl.ds((index_ref[0] ^ number) * blocks, blocks)],
            left.at[number],
        )
        for number in range(count)
    ]
    for copy in inward:
        copy.start()
    for come, go in zip(inward, outward):
        come.wait()
        go.start()
    for copy in outward:
        copy.wait()


def assemble(pieces, pair_index, after):
    count = len(pieces)
    shape, dtype = pieces[0].shape, pieces[0].dtype
    return pl.pallas_call(
        functools.partial(assemble_kernel, count),
        in_specs=[pl.BlockSpec(memory_space=pltpu.SMEM)] + [ANY] * (count + len(after)),
        out_specs=ANY,
        out_shape=jax.ShapeDtypeStruct((count * shape[0], *shape[1:]), dtype),
        scratch_shapes=[
            pltpu.VMEM((count, *shape), dtype),
            pltpu.SemaphoreType.DMA((count,)),
            pltpu.SemaphoreType.DMA((count,)),
        ],
        cost_estimate=pl.CostEstimate(
            flops=0, bytes_accessed=4 * count * pieces[0].size, transcendentals=0
        ),
        name="assemble",
    )(pair_index.reshape(1), *pieces, *after)


def gate_kernel(*refs):
    del refs


def gate(value, after):
    return pl.pallas_call(
        gate_kernel,
        in_specs=[ANY] * (1 + len(after)),
        out_specs=ANY,
        out_shape=jax.ShapeDtypeStruct(value.shape, value.dtype),
        input_output_aliases={0: 0},
        cost_estimate=pl.CostEstimate(flops=0, bytes_accessed=0, transcendentals=0),
        name="gate",
    )(value, *after)


GROUP = 2


def density_kernel(plan, distance_ref, *refs):
    occ_width, steps, slices, low, high, ends, segments, pair_count, starts, has_total = plan
    refs = list(refs)
    left_energy, right_energy = refs[:2]
    del refs[:2]
    local_refs = refs[:occ_width]
    del refs[:occ_width]
    held_refs = []
    for orbital in segments:
        held_refs.append([])
        for first, last in orbital:
            held_refs[-1].append((first, last, refs[:pair_count]))
            del refs[:pair_count]
    start_ref = refs.pop(0) if starts else None
    total_ref = refs.pop(0) if has_total else None
    out_ref = refs.pop(0)
    if starts:
        start_buffer, start_sem = refs[-2:]
        del refs[-2:]
    if ends:
        integrals, amplitudes, factors, remote_ref, sems = refs
    else:
        remote_ref, sems = refs
        integrals = out_ref
    width = held_refs[0][0][2][0].shape[1]
    step = pl.program_id(0)
    turns = (high - low) // GROUP

    def copy_of(ref, first, number, t):
        return pltpu.make_async_copy(
            ref.at[t - first],
            remote_ref.at[t, pl.ds(number * width, width)],
            sems.at[number, t],
        )

    @pl.when(step == 0)
    def _():
        wanted = []
        for orbital, parts in enumerate(held_refs):
            for first, last, blocks in parts:
                wanted.append((orbital, first, blocks, max(first, low), min(last, high)))
        if ends:
            for orbital, parts in enumerate(held_refs):
                for first, last, blocks in parts:
                    wanted.append((orbital, first, blocks, first, min(last, low)))
                    wanted.append((orbital, first, blocks, max(first, high), last))
        for orbital, first, blocks, begin, end in wanted:
            if begin < end:

                @pl.loop(begin, end)
                def _(t):
                    for position in range(steps):
                        for distance, ref in enumerate(blocks):
                            @pl.when(distance_ref[position] == distance)
                            def _():
                                copy_of(ref, first, orbital * steps + position, t).start()

    if starts:
        @pl.when(step == 0)
        def _():
            pltpu.make_async_copy(start_ref, start_buffer, start_sem).start()

    if ends:
        @pl.when(step == 0)
        def _():
            factors[...] = spin_scale / (left_energy[...] + right_energy[...])

    def wait_for(t):
        for number in range(len(held_refs) * steps):
            copy_of(held_refs[0][0][2][0], t, number, t).wait()

    @pl.when(step < turns)
    def _():
        now = low + step * GROUP
        for ahead in range(GROUP):
            wait_for(now + ahead)
        local = jnp.concatenate(
            [
                jnp.concatenate([ref[ahead] for ahead in range(GROUP)], axis=1)
                for ref in local_refs
            ],
            axis=0,
        )
        remote = jnp.concatenate([remote_ref[now + ahead] for ahead in range(GROUP)], axis=1)
        product = lax.dot_general(
            local, remote, (((1,), (1,)), ((), ())), preferred_element_type=jnp.float32
        )

        @pl.when(step == 0)
        def _():
            if starts:
                pltpu.make_async_copy(start_ref, start_buffer, start_sem).wait()
                integrals[...] = product + start_buffer[...]
            else:
                integrals[...] = product

        @pl.when(step > 0)
        def _():
            integrals[...] += product

        if ends:
            @pl.when(step == turns - 1)
            def _():
                amplitudes[...] = (integrals[...] * factors[...]).astype(jnp.bfloat16)

    if ends:
        @pl.when(step >= turns)
        def _():
            now = (step - turns) * GROUP
            for ahead in range(GROUP):
                @pl.when((now + ahead < low) | (now + ahead >= high))
                def _():
                    wait_for(now + ahead)

            remote = jnp.concatenate([remote_ref[now + ahead] for ahead in range(GROUP)], axis=1)
            product = jnp.dot(amplitudes[...], remote, preferred_element_type=jnp.float32)
            if has_total:
                product = product + total_ref[...]
            out_ref[...] = product.astype(out_ref.dtype)


def add_density(
    locals_, held, distances, left_energy, right_energy, span, ends, start=None, total=None
):
    occ_width, pair_count = len(locals_), len(held[0][0][2])
    steps = distances.shape[0]
    slices, width, aux_slice = locals_[0].shape
    rows, columns = occ_width * width, len(held) * steps * width
    low, high = span
    turns = (high - low) // GROUP
    base = low // GROUP
    in_specs = [
        pl.BlockSpec((rows, 1), lambda t, d: (0, 0)),
        pl.BlockSpec((1, columns), lambda t, d: (0, 0)),
    ]
    in_specs += [
        pl.BlockSpec(
            (GROUP, width, aux_slice), lambda t, d: (base + jnp.minimum(t, turns - 1), 0, 0)
        )
    ] * occ_width
    operands = [left_energy, right_energy, *locals_]
    for parts in held:
        for _, _, blocks in parts:
            operands += blocks
    in_specs += [ANY] * (len(operands) - len(in_specs))
    whole = pl.BlockSpec((rows, columns), lambda t, d: (0, 0))
    if start is not None:
        in_specs.append(ANY)
        operands.append(start)
    moved = 2 * (high - low) * aux_slice * rows + 2 * slices * aux_slice * columns
    scratch = [
        pltpu.VMEM((slices, columns, aux_slice), jnp.bfloat16),
        pltpu.SemaphoreType.DMA((len(held) * steps, slices)),
    ]
    if ends:
        out_spec = pl.BlockSpec((rows, GROUP * aux_slice), lambda t, d: (0, jnp.maximum(t - turns, 0)))
        out_shape = jax.ShapeDtypeStruct((rows, slices * aux_slice), jnp.bfloat16)
        scratch = [
            pltpu.VMEM((rows, columns), jnp.float32),
            pltpu.VMEM((rows, columns), jnp.bfloat16),
            pltpu.VMEM((rows, columns), jnp.float32),
        ] + scratch
        if total is not None:
            in_specs.append(out_spec)
            operands.append(total)
            moved += total.size * 2
    else:
        out_spec = whole
        out_shape = pltpu.VMEM((rows, columns), jnp.float32)
    moved += rows * max(columns * 4, slices * aux_slice * 2)
    if start is not None:
        scratch += [pltpu.VMEM((rows, columns), jnp.float32), pltpu.SemaphoreType.DMA]
    plan = (
        occ_width, steps, slices, low, high, ends,
        [[(first, last) for first, last, _ in parts] for parts in held],
        pair_count, start is not None, total is not None,
    )
    return pl.pallas_call(
        functools.partial(density_kernel, plan),
        grid_spec=pltpu.PrefetchScalarGridSpec(
            num_scalar_prefetch=1,
            grid=(turns + (slices // GROUP if ends else 0),),
            in_specs=in_specs,
            out_specs=out_spec,
            scratch_shapes=scratch,
        ),
        out_shape=out_shape,
        compiler_params=pltpu.CompilerParams(vmem_limit_bytes=VMEM_LIMIT),
        cost_estimate=pl.CostEstimate(
            flops=2 * rows * columns * aux_slice * (high - low + (slices if ends else 0)),
            bytes_accessed=moved,
            transcendentals=0,
        ),
        name="density" if ends else "integrals",
    )(distances, *operands)


def per_device(half_ints, vir_coeffs, occ_energy, vir_energy, roster):
    pair_count = lax.axis_size("pair")
    aux_count = lax.axis_size("aux")
    pair_index = lax.axis_index("pair")
    aux_index = lax.axis_index("aux")
    occ_rows, depth, aux_slice = half_ints.shape
    row_blocks = aux_count // pair_count
    occ_width = occ_rows // row_blocks
    step_count = roster.shape[1]

    coeff_rows = gather_coefficients(vir_coeffs)
    vir_width = coeff_rows.shape[0] // pair_count
    half = half_ints.reshape(row_blocks, occ_width, depth, aux_slice)

    sources = lax.dynamic_index_in_dim(roster, aux_index, 0, keepdims=False)
    occ_block = lax.dynamic_slice_in_dim(occ_energy, aux_index * occ_width, occ_width, 0)
    vir_block = lax.dynamic_slice_in_dim(vir_energy, pair_index * vir_width, vir_width, 0)
    left_energy = (vir_block[None, :] - occ_block[:, None]).reshape(-1, 1)
    source_energy = [
        lax.dynamic_slice_in_dim(vir_energy, sources[position] * vir_width, vir_width, 0)
        for position in range(step_count)
    ]

    def spread(block):
        blocks = [block]
        distance = 2
        while distance < pair_count:
            blocks += [swap(b, distance) for b in blocks]
            distance *= 2
        return blocks

    def share(blocks, after=None):
        if after is not None and len(blocks) > 1:
            blocks = blocks[:-1] + [gate(blocks[-1], after)]
        return [b for block in blocks for b in (block, swap(block, 1))]

    distant = tuple(range(2, pair_count))
    parts = [
        transform(coeff_rows, half, orbital, pair_index, distant)
        for orbital in range(1, occ_width)
    ]
    first = []
    for raw in spread(half[:, :1]):
        before = [] if first or not parts else [parts[0][-1]]
        own, other = transform(coeff_rows, raw, 0, pair_index, (0, 1), before)
        first += [own, swap(other, 1)]
    moved = [first] + [[swap(piece, d) for piece, d in zip(pieces, distant)] for pieces in parts]
    for orbital in range(1, occ_width):
        own, other = transform(coeff_rows, half, orbital, pair_index, (0, 1), moved[1][:1])
        moved[orbital] = [own, swap(other, 1)] + moved[orbital]

    locals_, far = [], []
    final = occ_width - 1
    middle = aux_count * 3 // 4
    for orbital in range(occ_width):
        sent = assemble(moved[orbital], pair_index, [])
        after = []
        if 0 < orbital < final:
            after += moved[orbital + 1][1:]
        if orbital > 1:
            after.append(far[orbital - 2][-1])
        if after:
            sent = gate(sent, after)
        local = lax.all_to_all(sent, "aux", split_axis=0, concat_axis=0, tiled=True)
        locals_.append(local)
        if orbital < occ_width - 1:
            far.append(spread(local))
    upper_rows = locals_[-1][middle:]
    halves = [spread(locals_[-1][:middle]), spread(upper_rows)]

    distances = (sources ^ pair_index).astype(jnp.int32)

    def right_of(orbitals):
        return jnp.concatenate(
            [energy - occ_block[orbital] for orbital in orbitals for energy in source_energy]
        ).reshape(1, -1)

    total = None
    everything = (0, aux_count)
    if occ_width > 1:
        first = range(occ_width - 1)
        held = [[(0, aux_count, share(far[orbital]))] for orbital in first]
        total = add_density(
            locals_, held, distances, left_energy, right_of(first), everything, True
        )
    right_energy = right_of([occ_width - 1])
    lower = (0, middle, share(halves[0], [upper_rows] if total is None else [total, upper_rows]))
    start = add_density(
        locals_, [[lower]], distances, left_energy, right_energy, (0, middle), False
    )
    upper = (middle, aux_count, share(halves[1], [start]))
    total = add_density(
        locals_, [[lower, upper]], distances, left_energy, right_energy, (middle, aux_count), True,
        start=start, total=total,
    )
    return jnp.transpose(total.reshape(occ_width, vir_width, -1), (1, 0, 2))


def solution(mesh):
    in_specs = (P("pair", None, "aux"), P(None, "aux"), P(), P(), P())
    out_specs = P("pair", "aux", None)
    return jax.shard_map(
        per_device, mesh=mesh, in_specs=in_specs, out_specs=out_specs, check_vma=False
    )
```

```python
import functools

import jax
import jax.numpy as jnp
from jax import lax
from jax.experimental import pallas as pl
from jax.experimental.pallas import tpu as pltpu
from jax.sharding import PartitionSpec as P

spin_scale = 1.3
VMEM_LIMIT = 56 * 1024 * 1024
ANY = pl.BlockSpec(memory_space=pl.ANY)


def swap(value, distance, axis="pair"):
    count = lax.axis_size(axis)
    pairs = [(source, source ^ distance) for source in range(count)]
    return lax.ppermute(value, axis, pairs)


def along(value, step):
    count = lax.axis_size("aux")
    pairs = [(a, a + 2 * step) for a in range(count) if 0 <= a + 2 * step < count]
    return lax.ppermute(value, "aux", pairs)


def place_kernel(line, index_ref, *refs):
    count = 2 * line - 1
    own_refs, mate_refs, out_ref, sems = refs[:count], refs[count:-2], refs[-2], refs[-1]
    here, side, core = index_ref[0], index_ref[1], index_ref[2]

    def each(action):
        for which, (half, piece_refs) in enumerate(((core, own_refs), (1 - core, mate_refs))):
            for number, ref in enumerate(piece_refs):
                shift = (number + 1) // 2
                row = here - shift if number % 2 else here + shift

                @pl.when((row >= 0) & (row < line))
                def _():
                    for slot in range(2):
                        action(
                            pltpu.make_async_copy(
                                ref.at[slot],
                                out_ref.at[row, side ^ slot, half],
                                sems.at[which, number, slot],
                            )
                        )

    each(lambda copy: copy.start())
    each(lambda copy: copy.wait())


def gather_coefficients(vir_coeffs):
    rows = jnp.transpose(vir_coeffs)
    part = rows.shape[0] // 2
    line = lax.axis_size("aux") // 2
    aux_index = lax.axis_index("aux")
    core = lax.axis_index("pair") % 2
    piece = lax.dynamic_slice_in_dim(rows, core * part, part, 0)
    both = jnp.stack([piece, swap(piece, 1, "aux")])
    own, mate = [both], [swap(both, 1)]
    below = above = both
    for _ in range(line - 1):
        below, above = along(below, 1), along(above, -1)
        own += [below, above]
        mate += [swap(below, 1), swap(above, 1)]
    depth = rows.shape[1]
    index = jnp.stack([aux_index // 2, aux_index % 2, core]).astype(jnp.int32)
    placed = pl.pallas_call(
        functools.partial(place_kernel, line),
        in_specs=[pl.BlockSpec(memory_space=pltpu.SMEM)]
        + [ANY] * (len(own) + len(mate)),
        out_specs=pl.BlockSpec(memory_space=pltpu.VMEM),
        out_shape=pltpu.VMEM((line, 2, 2, part, depth), rows.dtype),
        scratch_shapes=[pltpu.SemaphoreType.DMA((2, len(own), 2))],
        compiler_params=pltpu.CompilerParams(vmem_limit_bytes=VMEM_LIMIT),
        cost_estimate=pl.CostEstimate(
            flops=0, bytes_accessed=4 * line * 4 * part * depth, transcendentals=0
        ),
        name="place",
    )(index, *own, *mate)
    return placed.reshape(line * 4 * part, depth)


def transform_kernel(width, distances, index_ref, coeff_ref, half_ref, *refs):
    half = half_ref[0, 0]
    out_refs = refs[-len(distances) :]
    for distance, out_ref in zip(distances, out_refs):
        place = (index_ref[0] ^ distance) % (coeff_ref.shape[0] // width)
        start = pl.multiple_of(place * width, width)
        product = jnp.dot(
            coeff_ref[pl.ds(start, width), :], half, preferred_element_type=jnp.float32
        )
        out_ref[0] = product.astype(out_ref.dtype)


def transform(coeff_rows, half, orbital, pair_index, distances, after=()):
    pair_count = lax.axis_size("pair")
    blocks, _, depth, aux_slice = half.shape
    width = coeff_rows.shape[0] // pair_count
    near = 2 if max(distances) < 2 else pair_count
    count = len(distances)
    grid_spec = pltpu.PrefetchScalarGridSpec(
        num_scalar_prefetch=1,
        grid=(blocks,),
        in_specs=[
            pl.BlockSpec((near * width, depth), lambda b, index: (index[0] // near, 0)),
            pl.BlockSpec((1, 1, depth, aux_slice), lambda b, index: (b, orbital, 0, 0)),
        ]
        + [ANY] * len(after),
        out_specs=[pl.BlockSpec((1, width, aux_slice), lambda b, index: (b, 0, 0))] * count,
    )
    return pl.pallas_call(
        functools.partial(transform_kernel, width, distances),
        grid_spec=grid_spec,
        out_shape=[jax.ShapeDtypeStruct((blocks, width, aux_slice), jnp.bfloat16)] * count,
        compiler_params=pltpu.CompilerParams(vmem_limit_bytes=VMEM_LIMIT - 2 * 1024 * 1024),
        cost_estimate=pl.CostEstimate(
            flops=2 * blocks * count * width * depth * aux_slice,
            bytes_accessed=2 * (near * width * depth + blocks * (depth + count * width) * aux_slice),
            transcendentals=0,
        ),
        name="transform",
    )(pair_index.reshape(1), coeff_rows, half, *after)


def assemble_kernel(count, index_ref, *refs):
    piece_refs, (out_ref, held, arrived, left) = refs[:count], refs[-4:]
    blocks = held.shape[1]
    inward = [
        pltpu.make_async_copy(ref, held.at[number], arrived.at[number])
        for number, ref in enumerate(piece_refs)
    ]
    outward = [
        pltpu.make_async_copy(
            held.at[number],
            out_ref.at[pl.ds((index_ref[0] ^ number) * blocks, blocks)],
            left.at[number],
        )
        for number in range(count)
    ]
    for copy in inward:
        copy.start()
    for come, go in zip(inward, outward):
        come.wait()
        go.start()
    for copy in outward:
        copy.wait()


def assemble(pieces, pair_index, after):
    count = len(pieces)
    shape, dtype = pieces[0].shape, pieces[0].dtype
    return pl.pallas_call(
        functools.partial(assemble_kernel, count),
        in_specs=[pl.BlockSpec(memory_space=pltpu.SMEM)] + [ANY] * (count + len(after)),
        out_specs=ANY,
        out_shape=jax.ShapeDtypeStruct((count * shape[0], *shape[1:]), dtype),
        scratch_shapes=[
            pltpu.VMEM((count, *shape), dtype),
            pltpu.SemaphoreType.DMA((count,)),
            pltpu.SemaphoreType.DMA((count,)),
        ],
        cost_estimate=pl.CostEstimate(
            flops=0, bytes_accessed=4 * count * pieces[0].size, transcendentals=0
        ),
        name="assemble",
    )(pair_index.reshape(1), *pieces, *after)


def gate_kernel(*refs):
    del refs


def gate(value, after):
    return pl.pallas_call(
        gate_kernel,
        in_specs=[ANY] * (1 + len(after)),
        out_specs=ANY,
        out_shape=jax.ShapeDtypeStruct(value.shape, value.dtype),
        input_output_aliases={0: 0},
        cost_estimate=pl.CostEstimate(flops=0, bytes_accessed=0, transcendentals=0),
        name="gate",
    )(value, *after)


GROUP = 2


def density_kernel(plan, distance_ref, *refs):
    occ_width, steps, slices, low, high, ends, segments, pair_count, starts, has_total = plan
    refs = list(refs)
    left_energy, right_energy = refs[:2]
    del refs[:2]
    local_refs = refs[:occ_width]
    del refs[:occ_width]
    held_refs = []
    for orbital in segments:
        held_refs.append([])
        for first, last in orbital:
            held_refs[-1].append((first, last, refs[:pair_count]))
            del refs[:pair_count]
    start_ref = refs.pop(0) if starts else None
    total_ref = refs.pop(0) if has_total else None
    out_ref = refs.pop(0)
    if starts:
        start_buffer, start_sem = refs[-2:]
        del refs[-2:]
    if ends:
        integrals, amplitudes, remote_ref, sems = refs
    else:
        remote_ref, sems = refs
        integrals = out_ref
    width = held_refs[0][0][2][0].shape[1]
    step = pl.program_id(0)
    turns = (high - low) // GROUP

    def copy_of(ref, first, number, t):
        return pltpu.make_async_copy(
            ref.at[t - first],
            remote_ref.at[t, pl.ds(number * width, width)],
            sems.at[number, t],
        )

    @pl.when(step == 0)
    def _():
        wanted = []
        for orbital, parts in enumerate(held_refs):
            for first, last, blocks in parts:
                wanted.append((orbital, first, blocks, max(first, low), min(last, high)))
        if ends:
            for orbital, parts in enumerate(held_refs):
                for first, last, blocks in parts:
                    wanted.append((orbital, first, blocks, first, min(last, low)))
                    wanted.append((orbital, first, blocks, max(first, high), last))
        for orbital, first, blocks, begin, end in wanted:
            if begin < end:

                @pl.loop(begin, end)
                def _(t):
                    for position in range(steps):
                        for distance, ref in enumerate(blocks):
                            @pl.when(distance_ref[position] == distance)
                            def _():
                                copy_of(ref, first, orbital * steps + position, t).start()

    if starts:
        @pl.when(step == 0)
        def _():
            pltpu.make_async_copy(start_ref, start_buffer, start_sem).start()

    def wait_for(t):
        for number in range(len(held_refs) * steps):
            copy_of(held_refs[0][0][2][0], t, number, t).wait()

    @pl.when(step < turns)
    def _():
        now = low + step * GROUP
        for ahead in range(GROUP):
            wait_for(now + ahead)
        local = jnp.concatenate(
            [
                jnp.concatenate([ref[ahead] for ahead in range(GROUP)], axis=1)
                for ref in local_refs
            ],
            axis=0,
        )
        remote = jnp.concatenate([remote_ref[now + ahead] for ahead in range(GROUP)], axis=1)
        product = lax.dot_general(
            local, remote, (((1,), (1,)), ((), ())), preferred_element_type=jnp.float32
        )

        @pl.when(step == 0)
        def _():
            if starts:
                pltpu.make_async_copy(start_ref, start_buffer, start_sem).wait()
                integrals[...] = product + start_buffer[...]
            else:
                integrals[...] = product

        @pl.when(step > 0)
        def _():
            integrals[...] += product

        if ends:
            @pl.when(step == turns - 1)
            def _():
                gap = left_energy[...] + right_energy[...]
                amplitudes[...] = (spin_scale * integrals[...] / gap).astype(jnp.bfloat16)

    if ends:
        @pl.when(step >= turns)
        def _():
            now = (step - turns) * GROUP
            for ahead in range(GROUP):
                @pl.when((now + ahead < low) | (now + ahead >= high))
                def _():
                    wait_for(now + ahead)

            remote = jnp.concatenate([remote_ref[now + ahead] for ahead in range(GROUP)], axis=1)
            product = jnp.dot(amplitudes[...], remote, preferred_element_type=jnp.float32)
            if has_total:
                product = product + total_ref[...]
            out_ref[...] = product.astype(out_ref.dtype)


def add_density(
    locals_, held, distances, left_energy, right_energy, span, ends, start=None, total=None
):
    occ_width, pair_count = len(locals_), len(held[0][0][2])
    steps = distances.shape[0]
    slices, width, aux_slice = locals_[0].shape
    rows, columns = occ_width * width, len(held) * steps * width
    low, high = span
    turns = (high - low) // GROUP
    base = low // GROUP
    in_specs = [
        pl.BlockSpec((rows, 1), lambda t, d: (0, 0)),
        pl.BlockSpec((1, columns), lambda t, d: (0, 0)),
    ]
    in_specs += [
        pl.BlockSpec(
            (GROUP, width, aux_slice), lambda t, d: (base + jnp.minimum(t, turns - 1), 0, 0)
        )
    ] * occ_width
    operands = [left_energy, right_energy, *locals_]
    for parts in held:
        for _, _, blocks in parts:
            operands += blocks
    in_specs += [ANY] * (len(operands) - len(in_specs))
    whole = pl.BlockSpec((rows, columns), lambda t, d: (0, 0))
    if start is not None:
        in_specs.append(ANY)
        operands.append(start)
    moved = 2 * (high - low) * aux_slice * rows + 2 * slices * aux_slice * columns
    scratch = [
        pltpu.VMEM((slices, columns, aux_slice), jnp.bfloat16),
        pltpu.SemaphoreType.DMA((len(held) * steps, slices)),
    ]
    if ends:
        out_spec = pl.BlockSpec((rows, GROUP * aux_slice), lambda t, d: (0, jnp.maximum(t - turns, 0)))
        out_shape = jax.ShapeDtypeStruct((rows, slices * aux_slice), jnp.bfloat16)
        scratch = [
            pltpu.VMEM((rows, columns), jnp.float32),
            pltpu.VMEM((rows, columns), jnp.bfloat16),
        ] + scratch
        if total is not None:
            in_specs.append(out_spec)
            operands.append(total)
            moved += total.size * 2
    else:
        out_spec = whole
        out_shape = jax.ShapeDtypeStruct((rows, columns), jnp.float32)
    moved += out_shape.size * out_shape.dtype.itemsize
    if start is not None:
        scratch += [pltpu.VMEM((rows, columns), jnp.float32), pltpu.SemaphoreType.DMA]
    plan = (
        occ_width, steps, slices, low, high, ends,
        [[(first, last) for first, last, _ in parts] for parts in held],
        pair_count, start is not None, total is not None,
    )
    return pl.pallas_call(
        functools.partial(density_kernel, plan),
        grid_spec=pltpu.PrefetchScalarGridSpec(
            num_scalar_prefetch=1,
            grid=(turns + (slices // GROUP if ends else 0),),
            in_specs=in_specs,
            out_specs=out_spec,
            scratch_shapes=scratch,
        ),
        out_shape=out_shape,
        compiler_params=pltpu.CompilerParams(vmem_limit_bytes=VMEM_LIMIT),
        cost_estimate=pl.CostEstimate(
            flops=2 * rows * columns * aux_slice * (high - low + (slices if ends else 0)),
            bytes_accessed=moved,
            transcendentals=0,
        ),
        name="density" if ends else "integrals",
    )(distances, *operands)


def per_device(half_ints, vir_coeffs, occ_energy, vir_energy, roster):
    pair_count = lax.axis_size("pair")
    aux_count = lax.axis_size("aux")
    pair_index = lax.axis_index("pair")
    aux_index = lax.axis_index("aux")
    occ_rows, depth, aux_slice = half_ints.shape
    row_blocks = aux_count // pair_count
    occ_width = occ_rows // row_blocks
    step_count = roster.shape[1]

    coeff_rows = gather_coefficients(vir_coeffs)
    vir_width = coeff_rows.shape[0] // pair_count
    half = half_ints.reshape(row_blocks, occ_width, depth, aux_slice)

    sources = lax.dynamic_index_in_dim(roster, aux_index, 0, keepdims=False)
    occ_block = lax.dynamic_slice_in_dim(occ_energy, aux_index * occ_width, occ_width, 0)
    vir_block = lax.dynamic_slice_in_dim(vir_energy, pair_index * vir_width, vir_width, 0)
    left_energy = (vir_block[None, :] - occ_block[:, None]).reshape(-1, 1)
    source_energy = [
        lax.dynamic_slice_in_dim(vir_energy, sources[position] * vir_width, vir_width, 0)
        for position in range(step_count)
    ]

    def spread(block):
        blocks = [block]
        distance = 2
        while distance < pair_count:
            blocks += [swap(b, distance) for b in blocks]
            distance *= 2
        return blocks

    def share(blocks, after=None):
        if after is not None and len(blocks) > 1:
            blocks = blocks[:-1] + [gate(blocks[-1], after)]
        return [b for block in blocks for b in (block, swap(block, 1))]

    distant = tuple(range(2, pair_count))
    parts = [
        transform(coeff_rows, half, orbital, pair_index, distant)
        for orbital in range(1, occ_width)
    ]
    first = []
    for raw in spread(half[:, :1]):
        before = [] if first or not parts else [parts[0][-1]]
        own, other = transform(coeff_rows, raw, 0, pair_index, (0, 1), before)
        first += [own, swap(other, 1)]
    moved = [first] + [[swap(piece, d) for piece, d in zip(pieces, distant)] for pieces in parts]
    for orbital in range(1, occ_width):
        own, other = transform(coeff_rows, half, orbital, pair_index, (0, 1), moved[1][:1])
        moved[orbital] = [own, swap(other, 1)] + moved[orbital]

    locals_, far = [], []
    final = occ_width - 1
    middle = aux_count * 3 // 4
    for orbital in range(occ_width):
        sent = assemble(moved[orbital], pair_index, [])
        after = []
        if 0 < orbital < final:
            after += moved[orbital + 1][1:]
        if orbital > 1:
            after.append(far[orbital - 2][-1])
        if after:
            sent = gate(sent, after)
        local = lax.all_to_all(sent, "aux", split_axis=0, concat_axis=0, tiled=True)
        locals_.append(local)
        if orbital < occ_width - 1:
            far.append(spread(local))
    upper_rows = locals_[-1][middle:]
    halves = [spread(locals_[-1][:middle]), spread(upper_rows)]

    distances = (sources ^ pair_index).astype(jnp.int32)

    def right_of(orbitals):
        return jnp.concatenate(
            [energy - occ_block[orbital] for orbital in orbitals for energy in source_energy]
        ).reshape(1, -1)

    total = None
    everything = (0, aux_count)
    if occ_width > 1:
        first = range(occ_width - 1)
        held = [[(0, aux_count, share(far[orbital]))] for orbital in first]
        total = add_density(
            locals_, held, distances, left_energy, right_of(first), everything, True
        )
    right_energy = right_of([occ_width - 1])
    lower = (0, middle, share(halves[0], [upper_rows] if total is None else [total, upper_rows]))
    start = add_density(
        locals_, [[lower]], distances, left_energy, right_energy, (0, middle), False
    )
    upper = (middle, aux_count, share(halves[1], [start]))
    total = add_density(
        locals_, [[lower, upper]], distances, left_energy, right_energy, (middle, aux_count), True,
        start=start, total=total,
    )
    return jnp.transpose(total.reshape(occ_width, vir_width, -1), (1, 0, 2))


def solution(mesh):
    in_specs = (P("pair", None, "aux"), P(None, "aux"), P(), P(), P())
    out_specs = P("pair", "aux", None)
    return jax.shard_map(
        per_device, mesh=mesh, in_specs=in_specs, out_specs=out_specs, check_vma=False
    )
```
